256 devices in a mesh: seq: 64 (over y, z, core), row: 4 (over x).
Axes of the slice: x: 4, y: 4, z: 8, core: 2. Of those that a mesh axis runs over, the one named last changes fastest.
Arguments:
- hidden: bfloat16 [512, 64, 5120], P(None, 'seq', 'row'), may hold values from -120 to 120
- modulation: float32 [64, 2, 5120], P(None, None, 'row'), may hold values from -3 to 3
- projection: bfloat16 [5120, 64], P('row'), may hold values from -0.078125 to 0.078125
- projection_bias: float32 [64], replicated, may hold values from -3 to 3
- input_kernel: bfloat16 [27, 16, 384], replicated, may hold values from -0.3125 to 0.3125
- input_bias: float32 [384], replicated, may hold values from -2 to 2
- norm_gain: float32 [384], replicated, may hold values from 0.1 to 1.9
- block_kernel: bfloat16 [27, 384, 384], replicated, may hold values from -0.0625 to 0.0625
- block_bias: float32 [384], replicated, may hold values from -2 to 2
- frame_counts: int32 [64], replicated, may hold values from 1 to 81, 512 in all
- decoder_plan: int32 [512], replicated, may hold values from 0 to 255, as said below
Outputs:
- decoded: bfloat16 [1024, 2, 128, 384], P(('seq', 'row'))
The draws below stay inside these ranges and needn't reach their ends.
Inputs may be any that keep to these rules, and one draw needn't show every extreme that they name: `decoder_plan`: each decoder device is named by at most 4 frames, and one is named by exactly 4. `frame_counts`: the counts sum to 512 and the largest is 81.
All inputs are finite; a program needn't handle non-finite values.
Results may differ from the reference program's by a relative error of at most 0.0058.
Values may be sent and summed in bfloat16 or wider, within the bound.
A program may use at most 256 MiB of HBM per device.

```python
import math
import jax
import jax.numpy as jnp
import numpy as np
from jax import lax

D = 5120
Z = 16
C = 384
TCOLS = 64
LCOLS = 128
FRAMES = 512
REQ = 64
MOST = 81
CAP = 4
DECODERS = 256


def draw_hidden(key, part):
    key = jax.random.fold_in(key, 5)
    streams = jax.random.split(key, 2)
    rising = 1.0 + 2.0 * jnp.arange(D, dtype=jnp.float32) / (D - 1)
    columns = rising * jnp.exp(jax.random.uniform(streams[0], (D,), jnp.float32, -0.6, 0.6))
    values = jnp.clip(jax.random.normal(streams[1], (FRAMES, TCOLS, D), jnp.float32), -6.0, 6.0) * columns
    return values.astype(jnp.bfloat16)


def draw_decoder_plan(key, part):
    key = jax.random.fold_in(key, 11)
    streams = jax.random.split(key, 3)
    total_slots = DECODERS * CAP
    slot_ids = jnp.arange(total_slots, dtype=jnp.int32)
    busiest = jax.random.randint(streams[0], (), 0, DECODERS, dtype=jnp.int32)
    shuffled = jax.random.permutation(streams[1], total_slots).astype(jnp.int32)
    priority = jnp.where(slot_ids // CAP == busiest, slot_ids % CAP - CAP, shuffled)
    chosen = jnp.argsort(priority, stable=True)[:FRAMES].astype(jnp.int32)
    mixed = jax.random.permutation(streams[2], chosen)
    return (mixed // CAP).astype(jnp.int32)


def levels(rng, extent, cuts, smallest, high):
    def one(axis_at, shards_of):
        heights = jax.random.uniform(jax.random.fold_in(jax.random.fold_in(rng, 6), axis_at), (shards_of,), jnp.float32, smallest / len(cuts), high / len(cuts))
        return jnp.repeat(jnp.exp(heights), extent[axis_at] // shards_of).reshape((-1,) + (1,) * (len(extent) - axis_at - 1))

    loudness = one(*cuts[0])
    for cut in cuts[1:]:
        loudness = loudness * one(*cut)
    return loudness


def profile(amount, total, reach, skew):
    weights = [(1 << 20) // math.isqrt(standing ** skew) + 1 for standing in range(2, amount + 1)]
    spare, holding = total - reach - (amount - 1), [1] * (amount - 1)
    while spare > 0:
        candidates = [i for i in range(amount - 1) if holding[i] < reach]
        whole, budget = sum([weights[i] for i in candidates]), spare
        for i in candidates:
            extra = min(reach - holding[i], max(1, budget * weights[i] // whole), spare)
            holding[i] = holding[i] + extra
            spare = spare - extra
    return np.array([reach] + holding)


def ragged_sizes(own_key, number_of, total, bound, slope):
    if number_of == 2:
        one = jax.random.randint(own_key, (), max(1, total - bound), min(bound, total - 1) + 1)
        return jnp.stack([one, total - one])
    lengths = jnp.asarray(profile(number_of, total, bound, slope), jnp.int32)
    twos = (number_of - 1) // 2
    donor, receiver = lengths[1:1 + 2 * twos:2], lengths[2:2 + 2 * twos:2]
    room = jnp.minimum(donor - 1, bound - receiver)
    moved = jax.random.randint(jax.random.fold_in(own_key, 1), (twos,), 0, 1 << 20) % (room + 1)
    lengths = lengths.at[1:1 + 2 * twos:2].set(donor - moved).at[2:2 + 2 * twos:2].set(receiver + moved)
    return lengths[jax.random.permutation(jax.random.fold_in(own_key, 2), number_of)]


def centred(own_key, dims, scale, bound, shards=(), kind=jnp.bfloat16):
    drawn = scale * jax.random.normal(own_key, dims, jnp.float32)
    if shards:
        drawn = drawn * levels(own_key, dims, shards, -0.22, 0.18)
    return jnp.clip(drawn, -bound, bound).astype(kind)


def setup_inputs(seed: int = 0) -> dict:
    splits = jax.random.split(jax.random.key(seed), 12)
    return {
        "hidden": draw_hidden(jax.random.fold_in(splits[11], 71), 0),
        "modulation": centred(splits[1], (REQ, 2, D), 0.5, 3.0, ((2, 4),), jnp.float32),
        "projection": centred(splits[2], (D, 4 * Z), D ** -0.5, 0.078125, ((0, 4),)),
        "projection_bias": centred(splits[3], (4 * Z,), 0.5, 3.0, (), jnp.float32),
        "input_kernel": centred(splits[4], (27, Z, C), (27 * Z) ** -0.5, 0.3125),
        "input_bias": centred(splits[5], (C,), 0.3, 2.0, (), jnp.float32),
        "norm_gain": jnp.clip(1.0 + 0.18 * jax.random.normal(splits[6], (C,), jnp.float32), 0.1, 1.9),
        "block_kernel": centred(splits[7], (27, C, C), (27 * C) ** -0.5, 0.0625),
        "block_bias": centred(splits[8], (C,), 0.3, 2.0, (), jnp.float32),
        "frame_counts": ragged_sizes(splits[9], REQ, FRAMES, MOST, 2).astype(jnp.int32),
        "decoder_plan": draw_decoder_plan(jax.random.fold_in(splits[11], 71), 0),
    }


EPSILON = 1e-06

def request_layout(frame_counts):
    timeline = jnp.arange(FRAMES, dtype=jnp.int32)
    request_ends = jnp.cumsum(frame_counts).astype(jnp.int32)
    passed = (request_ends[None, :] <= timeline[:, None]).astype(jnp.int32)
    request_of = lax.optimization_barrier(jnp.sum(passed, axis=1)).astype(jnp.int32)
    first_frame = lax.optimization_barrier(jnp.sum(passed * frame_counts[None, :], axis=1)).astype(jnp.int32)
    return (timeline, request_of, first_frame)

def causal_conv(source, kernel, first_frame):
    frames_in, rows_in, cols_in, channels_in = source.shape
    padded = jnp.pad(source.astype(jnp.float32), ((2, 0), (1, 1), (1, 1), (0, 0)))
    timeline = jnp.arange(frames_in, dtype=jnp.int32)
    summed = jnp.zeros((frames_in, rows_in, cols_in, kernel.shape[2]), jnp.float32)
    for time_tap in range(3):
        allowed = (timeline - 2 + time_tap >= first_frame).astype(jnp.float32)[:, None, None, None]
        for row_tap in range(3):
            for col_tap in range(3):
                sliced = padded[time_tap:time_tap + frames_in, row_tap:row_tap + rows_in, col_tap:col_tap + cols_in]
                weights = kernel[9 * time_tap + 3 * row_tap + col_tap].astype(jnp.float32)
                product = jnp.dot(sliced.reshape(-1, channels_in), weights, preferred_element_type=jnp.float32)
                summed = summed + product.reshape(summed.shape) * allowed
    return summed

def reference(hidden, modulation, projection, projection_bias, input_kernel, input_bias, norm_gain, block_kernel, block_bias, frame_counts, decoder_plan):
    timeline, request_of, first_frame = request_layout(frame_counts)
    values = hidden.astype(jnp.float32)
    average = lax.optimization_barrier(jnp.mean(values, axis=-1, keepdims=True))
    variance = lax.optimization_barrier(jnp.mean(values * values, axis=-1, keepdims=True)) - average * average
    inverse = lax.rsqrt(variance + EPSILON)
    shifts = modulation[request_of, 0, :][:, None, :]
    scales = modulation[request_of, 1, :][:, None, :]
    normed = (values - average) * inverse * (1.0 + scales) + shifts
    tokens = jnp.einsum('ftd,dk->ftk', normed, projection.astype(jnp.float32), precision=lax.Precision.HIGHEST) + projection_bias
    latent = tokens.astype(jnp.bfloat16).reshape(FRAMES, TCOLS, 2, 2, Z)
    latent = jnp.transpose(latent, (0, 2, 1, 3, 4)).reshape(FRAMES, 2, LCOLS, Z)
    features = (causal_conv(latent, input_kernel, first_frame) + input_bias).astype(jnp.bfloat16)
    widened = features.astype(jnp.float32)
    normalized = widened * lax.rsqrt(lax.optimization_barrier(jnp.mean(widened * widened, axis=-1, keepdims=True)) + EPSILON) * norm_gain
    activated = jax.nn.silu(normalized).astype(jnp.bfloat16)
    framed = (widened + block_bias + causal_conv(activated, block_kernel, first_frame)).astype(jnp.bfloat16)
    same_device = decoder_plan[:, None] == decoder_plan[None, :]
    earlier = timeline[None, :] < timeline[:, None]
    ranking = lax.optimization_barrier(jnp.sum(jnp.logical_and(same_device, earlier), axis=1)).astype(jnp.int32)
    slot_of = (decoder_plan * CAP + ranking).astype(jnp.int32)
    decoded = jnp.zeros((DECODERS * CAP, 2, LCOLS, C), jnp.bfloat16).at[slot_of].set(framed)
    return decoded
```

```python
import functools

import jax
import jax.numpy as jnp
from jax import lax
from jax.experimental import pallas as pl
from jax.experimental.pallas import tpu as pltpu
from jax.sharding import PartitionSpec as P

MESH = pl.DeviceIdType.MESH
F32 = jnp.float32
BF16 = jnp.bfloat16

D = 5120
DL = 1280
Z = 16
C = 384
CAP = 4
FRAMES = 512
REQ = 64
SEQ = 64
ROW = 4
QF = FRAMES // ROW
EPSILON = 1e-06


def iota(shape, dim):
    return lax.broadcasted_iota(jnp.int32, shape, dim)


def split_bf16(x):
    high = x.astype(BF16)
    return high, (x - high.astype(F32)).astype(BF16)


def dot(a, b):
    return lax.dot_general(a, b, (((1,), (0,)), ((), ())), preferred_element_type=F32)


def dot_nt(a, b):
    return lax.dot_general(a, b, (((1,), (1,)), ((), ())), preferred_element_type=F32)


def to_rows(column, eye):
    return jnp.sum(jnp.where(eye, column, 0.0), axis=0, keepdims=True)


def to_columns(row, eye):
    return jnp.sum(jnp.where(eye, row, 0.0), axis=1, keepdims=True)


def head_kernel(
    hid_hbm,
    mod_hbm,
    proj_hbm,
    bias_hbm,
    counts_hbm,
    plan_hbm,
    y_ref,
    mask_ref,
    hid,
    mod,
    proj,
    bias,
    counts,
    plan,
    stats,
    stats_in,
    part,
    tok,
    tok_in,
    lat,
    spread,
    onehot,
    sendbuf,
    recv,
    local_sem,
    stat_send,
    stat_recv,
    tok_send,
    tok_recv,
    lat_send,
    lat_recv,
    out_send,
    out_recv,
):
    my_seq = lax.axis_index("seq")
    my_row = lax.axis_index("row")

    loads = [
        pltpu.make_async_copy(counts_hbm, counts, local_sem.at[0]),
        pltpu.make_async_copy(plan_hbm, plan, local_sem.at[1]),
        pltpu.make_async_copy(proj_hbm, proj, local_sem.at[2]),
        pltpu.make_async_copy(mod_hbm, mod, local_sem.at[3]),
        pltpu.make_async_copy(bias_hbm, bias, local_sem.at[4]),
    ]
    hid_loads = [
        pltpu.make_async_copy(
            hid_hbm.at[pl.ds(QF * q, QF)], hid.at[pl.ds(QF * q, QF)], local_sem.at[5 + q]
        )
        for q in range(ROW)
    ]
    for copy in hid_loads + loads:
        copy.start()

    barrier = pltpu.get_barrier_semaphore()
    for i in range(1, ROW):
        pl.semaphore_signal(
            barrier,
            inc=1,
            device_id=(my_seq, lax.rem(my_row + i, ROW)),
            device_id_type=MESH,
        )

    def greet(i, carry):
        pl.semaphore_signal(
            barrier,
            inc=1,
            device_id=(lax.rem(my_seq + i, SEQ), my_row),
            device_id_type=MESH,
        )
        return carry

    lax.fori_loop(1, SEQ, greet, 0)

    eye = iota((QF, QF), 0) == iota((QF, QF), 1)

    means = []
    for q in range(ROW):
        hid_loads[q].wait()
        h = hid[QF * q : QF * (q + 1), :].astype(F32)
        one = jnp.sum(h, axis=1, keepdims=True)
        two = jnp.sum(h * h, axis=1, keepdims=True)
        means.append(one / DL)
        stats[q : q + 1, :] = to_rows(one, eye)
        stats[ROW + q : ROW + q + 1, :] = to_rows(two, eye)

    pl.semaphore_wait(barrier, ROW - 1 + SEQ - 1)
    stat_copies = []
    for i in range(1, ROW):
        copy = pltpu.make_async_remote_copy(
            src_ref=stats,
            dst_ref=stats_in.at[i - 1],
            send_sem=stat_send.at[i - 1],
            recv_sem=stat_recv.at[i - 1],
            device_id=(my_seq, lax.rem(my_row + i, ROW)),
            device_id_type=MESH,
        )
        copy.start()
        stat_copies.append(copy)

    for copy in loads:
        copy.wait()
    counts_row = counts[...].astype(F32)
    square = (REQ, REQ)
    counts_col = jnp.sum(
        jnp.where(iota(square, 0) == iota(square, 1), counts_row, 0.0), axis=1, keepdims=True
    )
    ends_col = jnp.sum(
        jnp.where(iota(square, 1) <= iota(square, 0), counts_row, 0.0), axis=1, keepdims=True
    )
    starts_col = ends_col - counts_col
    wide = (REQ, 2 * REQ)
    request_lane = lax.rem(iota(wide, 1), REQ)
    ends_row = jnp.sum(
        jnp.where(iota(wide, 0) <= request_lane, counts_col, 0.0), axis=0, keepdims=True
    )
    starts_row = jnp.sum(
        jnp.where(iota(wide, 0) < request_lane, counts_col, 0.0), axis=0, keepdims=True
    )

    lanes = (Z * 4, 2 * Z * 4)
    lane = lax.rem(iota(lanes, 1), 4 * Z)
    wanted = lax.rem(lane // Z, 2) * (2 * Z) + (lane // (2 * Z)) * Z + lax.rem(lane, Z)
    reorder = jnp.where(iota(lanes, 0) == wanted, 1.0, 0.0).astype(BF16)
    weight = lax.dot_general(
        proj[...], reorder, (((0,), (0,)), ((), ())), preferred_element_type=F32
    ).astype(BF16)
    bias_hi, bias_lo = split_bf16(jnp.broadcast_to(bias[...], (16, 4 * Z)))
    bias_lo2 = (
        jnp.broadcast_to(bias[...], (16, 4 * Z)) - bias_hi.astype(F32) - bias_lo.astype(F32)
    ).astype(BF16)
    bias_row = (dot(bias_hi, reorder) + dot(bias_lo, reorder) + dot(bias_lo2, reorder))[0:1, :]

    gain_hi, gain_lo = split_bf16(1.0 + mod[:, 1, :])
    shift_hi, shift_lo = split_bf16(mod[:, 0, :])
    gain_weight = dot(gain_hi, weight) + dot(gain_lo, weight)
    shift_weight = dot(shift_hi, weight) + dot(shift_lo, weight)
    gains = jnp.concatenate([gain_hi, gain_lo], axis=0)
    per_request = jnp.concatenate([gain_weight, shift_weight], axis=1)
    request_hi, request_lo = split_bf16(per_request)
    per_request = jnp.concatenate([request_hi, request_lo], axis=0)

    for q in range(ROW):
        frame = (iota((QF, 2 * REQ), 0) + QF * q).astype(F32)
        member = jnp.where(
            jnp.logical_and(frame >= starts_row, frame < ends_row), 1.0, 0.0
        ).astype(BF16)
        gain = dot(member, gains)
        h = hid[QF * q : QF * (q + 1), :].astype(F32)
        x_hi, x_lo = split_bf16((h - means[q]) * gain)
        part[QF * q : QF * (q + 1), 0:128] = dot(x_hi, weight) + dot(x_lo, weight)
        part[QF * q : QF * (q + 1), 128:384] = dot(member, per_request)

    plan_row = plan[...]
    plan_f32 = plan_row.astype(F32)
    frame_row = iota((1, FRAMES), 1)
    frame_f32 = frame_row.astype(F32)
    rank = jnp.zeros((1, FRAMES), F32)
    for q in range(ROW):
        plan_col = to_columns(plan_f32[:, QF * q : QF * (q + 1)], eye)
        before = iota((QF, FRAMES), 0) + QF * q < iota((QF, FRAMES), 1)
        rank += jnp.sum(
            jnp.where(jnp.logical_and(plan_col == plan_f32, before), 1.0, 0.0),
            axis=0,
            keepdims=True,
        )
    code = jnp.where(
        plan_row - (plan_row // ROW) * ROW == my_row,
        (plan_row // ROW).astype(F32) * CAP + rank,
        -1.0,
    )
    by_request = (REQ, FRAMES)
    frame_of = iota(by_request, 1).astype(F32)
    first = jnp.sum(
        jnp.where(
            jnp.logical_and(frame_of >= starts_col, frame_of < ends_col), starts_col, 0.0
        ),
        axis=0,
        keepdims=True,
    )
    shifted = []
    for back in range(5):
        if back == 0:
            shifted.append(code)
            continue
        code_ahead = pltpu.roll(jnp.broadcast_to(code, (8, FRAMES)), FRAMES - back, 1)[0:1]
        first_ahead = pltpu.roll(jnp.broadcast_to(first, (8, FRAMES)), FRAMES - back, 1)[0:1]
        shifted.append(
            jnp.where(
                jnp.logical_and(first_ahead <= frame_f32, frame_row < FRAMES - back),
                code_ahead,
                -1.0,
            )
        )
    table = []
    for high in range(2):
        rows = iota((16, FRAMES), 0)
        place = lax.rem(rows, 4)
        picked = jnp.broadcast_to(shifted[1 - high], (16, FRAMES))
        for at in range(3):
            picked = jnp.where(place == at, shifted[4 - at - high], picked)
        table.append(picked - (rows // 4).astype(F32))
    table = jnp.concatenate(table, axis=1)

    own = jnp.where(table == (my_seq * CAP).astype(F32), 1.0, 0.0)
    mask_ref[0] = jnp.broadcast_to(
        jnp.sum(own[:, 0:FRAMES], axis=1, keepdims=True), (16, 128)
    )
    mask_ref[1] = jnp.broadcast_to(
        jnp.sum(own[:, FRAMES : 2 * FRAMES], axis=1, keepdims=True), (16, 128)
    )
    for s in range(SEQ):
        onehot[16 * s : 16 * (s + 1), :] = jnp.where(table == float(CAP * s), 1.0, 0.0).astype(
            BF16
        )

    for copy in stat_copies:
        copy.wait_recv()
    total = stats[...] + stats_in[0] + stats_in[1] + stats_in[2]
    average_row = total[0:ROW] / D
    inverse_row = lax.rsqrt(total[ROW : 2 * ROW] / D - average_row * average_row + EPSILON)
    half = iota((QF // 2, 128), 1) < 64
    for q in range(ROW):
        average = to_columns(average_row[q : q + 1], eye)
        inverse = to_columns(inverse_row[q : q + 1], eye)
        rows = slice(QF * q, QF * (q + 1))
        share = inverse * (
            part[rows, 0:128] + (means[q] - average) * part[rows, 128:256]
        ) + part[rows, 256:384]
        tok[q] = jnp.where(half, share[0 : QF // 2], share[QF // 2 : QF])
    tok_copies = []
    for i in range(1, ROW):
        peer = lax.rem(my_row + i, ROW)
        copy = pltpu.make_async_remote_copy(
            src_ref=tok.at[peer],
            dst_ref=tok_in.at[i - 1],
            send_sem=tok_send.at[i - 1],
            recv_sem=tok_recv.at[i - 1],
            device_id=(my_seq, peer),
            device_id_type=MESH,
        )
        copy.start()
        tok_copies.append(copy)
    for copy in tok_copies:
        copy.wait_recv()
    lat[my_row] = (
        tok[my_row] + tok_in[0] + tok_in[1] + tok_in[2] + bias_row
    ).astype(BF16)
    lat_copies = []
    for i in range(1, ROW):
        copy = pltpu.make_async_remote_copy(
            src_ref=lat.at[my_row],
            dst_ref=lat.at[my_row],
            send_sem=lat_send.at[i - 1],
            recv_sem=lat_recv.at[i - 1],
            device_id=(my_seq, lax.rem(my_row + i, ROW)),
            device_id_type=MESH,
        )
        copy.start()
        lat_copies.append(copy)
    for copy in lat_copies:
        copy.wait_recv()

    for q in range(ROW):
        here = lat[q].astype(F32)
        there = pltpu.roll(here, 64, 1)
        low, high = jnp.where(half, here, 0.0), jnp.where(half, 0.0, here)
        low_moved, high_moved = jnp.where(half, there, 0.0), jnp.where(half, 0.0, there)
        for at, block in (
            (QF * q, low),
            (QF * q + 64, low_moved),
            (FRAMES + QF * q, high_moved),
            (FRAMES + QF * q + 64, high),
        ):
            spread[at : at + 64, :] = block.astype(BF16)
    for block in range(4):
        rows = slice(256 * block, 256 * (block + 1))
        sendbuf[16 * block : 16 * (block + 1)] = (
            dot(onehot[rows, :], spread[...]).astype(BF16).reshape(16, 16, 128)
        )

    def post(i, carry):
        to = lax.rem(my_seq + i, SEQ)
        pltpu.make_async_remote_copy(
            src_ref=sendbuf.at[to],
            dst_ref=recv.at[my_seq],
            send_sem=out_send,
            recv_sem=out_recv,
            device_id=(to, my_row),
            device_id_type=MESH,
        ).start()
        return carry

    lax.fori_loop(1, SEQ, post, 0)
    recv[my_seq] = sendbuf[my_seq]

    moved = (256, 256)
    to_row, from_row = iota(moved, 0), iota(moved, 1)
    group = to_row // 16
    source = lax.rem(to_row, 16) * 16 + lax.rem(group, 4) * 4 + group // 4
    mover = jnp.where(from_row == source, 1.0, 0.0).astype(BF16)

    arrived = recv.at[pl.ds(0, SEQ - 1)]
    pltpu.make_async_copy(arrived, arrived, out_recv).wait()
    for block in range(4):
        got = recv[16 * block : 16 * (block + 1)].reshape(256, 128)
        y_ref[:, 16 * block : 16 * (block + 1), :] = (
            dot(mover, got).astype(BF16).reshape(16, 16, 128)
        )

    for copy in stat_copies + tok_copies + lat_copies:
        copy.wait_send()
    sent = sendbuf.at[pl.ds(0, SEQ - 1)]
    pltpu.make_async_copy(sent, sent, out_send).wait()


def tail_kernel(
    y_ref,
    mask_ref,
    ker1,
    bias1,
    gain,
    ker2_hbm,
    bias2,
    out_ref,
    taps,
    w1,
    lhs,
    acc,
    feat,
    sem,
):
    for t in range(3):
        for p in range(2):
            for e in range(3):
                for i in range(2):
                    pltpu.make_async_copy(
                        ker2_hbm.at[9 * t + 3 * (p - i + 1) + e],
                        taps.at[t, pl.ds((3 * p + e) * C, C), pl.ds(i * C, C)],
                        sem.at[t],
                    ).start()

    def fill(base, a, columns):
        for n, (position, q) in enumerate(columns):
            for i in range(2):
                for r in range(2):
                    e = position - r + 1
                    if 0 <= e <= 2:
                        block = ker1[9 * a + 3 * (q - i + 1) + e]
                    else:
                        block = jnp.zeros((Z, C), BF16)
                    w1[base + Z * n : base + Z * (n + 1), (2 * i + r) * C : (2 * i + r + 1) * C] = (
                        block
                    )

    own = [(0, 0), (0, 1), (1, 0), (1, 1)]
    rim = [(2, 0), (2, 1), (-1, 0), (-1, 1)]
    for base, a, columns in (
        (0, 0, own),
        (64, 1, own),
        (128, 0, rim),
        (192, 2, own),
        (256, 1, rim),
        (320, 2, rim),
    ):
        fill(base, a, columns)

    rows = CAP * SEQ
    column = lax.rem(iota((rows, 128), 0), SEQ)
    lane = iota((rows, 128), 1)

    def rims(v):
        right = jnp.where(column == SEQ - 1, 0.0, pltpu.roll(v, rows - 1, 0))
        left = jnp.where(column == 0, 0.0, pltpu.roll(v, 1, 0))
        return jnp.where(lax.rem(lane, 64) < 32, right, left)

    wide = [y_ref[CAP * t : CAP * (t + 1)].reshape(rows, 128).astype(F32) for t in range(4)]
    around = [rims(v) for v in wide]
    first_col = lax.rem(iota((rows, C), 0), SEQ) == 0
    last_col = lax.rem(iota((rows, C), 0), SEQ) == SEQ - 1
    bias1_row = bias1[...]
    gain_row = gain[...]

    def mask_of(t):
        which, row = ((0, 2), (0, 3), (1, 3))[t]
        return jnp.concatenate(
            [
                jnp.broadcast_to(mask_ref[which, 4 * k + row : 4 * k + row + 1, 0:1], (SEQ, 1))
                for k in range(CAP)
            ],
            axis=0,
        )

    for t in range(3):
        x = jnp.concatenate(
            [wide[t], jnp.where(lane < 64, around[t], wide[t + 1]), around[t + 1]], axis=1
        ).astype(BF16)
        live = mask_of(t)
        for p in range(2):
            both = dot(x, w1[:, 2 * p * C : 2 * (p + 1) * C])
            for r in range(2):
                f = (both[:, r * C : (r + 1) * C] + bias1_row).astype(BF16)
                v = f.astype(F32)
                if t == 2:
                    feat[:, (2 * p + r) * C : (2 * p + r + 1) * C] = f
                scale = lax.rsqrt(jnp.mean(v * v, axis=1, keepdims=True) + EPSILON) * live
                n = v * scale * gain_row
                a = 0.5 * n * (1.0 + jnp.tanh(0.5 * n))

                def put(side, e, value):
                    lhs[
                        t,
                        side * rows : (side + 1) * rows,
                        (3 * p + e) * C : (3 * p + e + 1) * C,
                    ] = value.astype(BF16)

                if r == 0:
                    put(0, 1, a)
                    put(1, 0, a)
                    put(1, 2, jnp.where(last_col, 0.0, pltpu.roll(a, rows - 1, 0)))
                else:
                    put(0, 2, a)
                    put(1, 1, a)
                    put(0, 0, jnp.where(first_col, 0.0, pltpu.roll(a, 1, 0)))
        pltpu.make_async_copy(taps.at[t], taps.at[t], sem.at[t]).wait()
        product = dot(lhs[t], taps[t])
        if t == 0:
            acc[...] = product
        else:
            acc[...] += product

    mixed = (2 * SEQ, 2 * SEQ)
    to_row, from_row = iota(mixed, 0), iota(mixed, 1)
    mixer = jnp.where(from_row == lax.rem(to_row, 2) * SEQ + to_row // 2, 1.0, 0.0).astype(BF16)
    bias2_row = bias2[...]
    for k in range(CAP):
        live = mask_ref[1, 4 * k + 3 : 4 * k + 4, 0:1]
        for i in range(2):
            halves = []
            for r in range(2):
                at = r * rows + k * SEQ
                halves.append(
                    (
                        (
                            feat[k * SEQ : (k + 1) * SEQ, (2 * i + r) * C : (2 * i + r + 1) * C].astype(
                                F32
                            )
                            + bias2_row
                            + acc[at : at + SEQ, i * C : (i + 1) * C]
                        )
                        * live
                    ).astype(BF16)
                )
            out_ref[k, i] = dot(mixer, jnp.concatenate(halves, axis=0)).astype(BF16)


def shards(
    hidden,
    modulation,
    projection,
    projection_bias,
    input_kernel,
    input_bias,
    norm_gain,
    block_kernel,
    block_bias,
    frame_counts,
    decoder_plan,
):
    any_space = pl.BlockSpec(memory_space=pl.ANY)
    vmem = pl.BlockSpec(memory_space=pltpu.VMEM)
    y, mask = pl.pallas_call(
        head_kernel,
        out_shape=(
            jax.ShapeDtypeStruct((16, SEQ, 128), BF16),
            jax.ShapeDtypeStruct((2, 16, 128), F32),
        ),
        in_specs=[any_space] * 6,
        out_specs=(vmem, vmem),
        scratch_shapes=[
            pltpu.VMEM((FRAMES, DL), BF16),
            pltpu.VMEM((REQ, 2, DL), F32),
            pltpu.VMEM((4 * Z, DL), BF16),
            pltpu.VMEM((1, 4 * Z), F32),
            pltpu.VMEM((1, REQ), jnp.int32),
            pltpu.VMEM((1, FRAMES), jnp.int32),
            pltpu.VMEM((2 * ROW, QF), F32),
            pltpu.VMEM((ROW - 1, 2 * ROW, QF), F32),
            pltpu.VMEM((FRAMES, 384), F32),
            pltpu.VMEM((ROW, QF // 2, 128), F32),
            pltpu.VMEM((ROW - 1, QF // 2, 128), F32),
            pltpu.VMEM((ROW, QF // 2, 128), BF16),
            pltpu.VMEM((2 * FRAMES, 128), BF16),
            pltpu.VMEM((16 * SEQ, 2 * FRAMES), BF16),
            pltpu.VMEM((SEQ, 16, 128), BF16),
            pltpu.VMEM((SEQ, 16, 128), BF16),
            pltpu.SemaphoreType.DMA((5 + ROW,)),
            pltpu.SemaphoreType.DMA((ROW - 1,)),
            pltpu.SemaphoreType.DMA((ROW - 1,)),
            pltpu.SemaphoreType.DMA((ROW - 1,)),
            pltpu.SemaphoreType.DMA((ROW - 1,)),
            pltpu.SemaphoreType.DMA((ROW - 1,)),
            pltpu.SemaphoreType.DMA((ROW - 1,)),
            pltpu.SemaphoreType.DMA,
            pltpu.SemaphoreType.DMA,
        ],
        compiler_params=pltpu.CompilerParams(
            collective_id=0, has_side_effects=True, vmem_limit_bytes=40 << 20
        ),
    )(
        hidden.reshape(FRAMES, DL),
        modulation,
        projection.T,
        projection_bias.reshape(1, 4 * Z),
        frame_counts.reshape(1, REQ),
        decoder_plan.reshape(1, FRAMES),
    )
    return pl.pallas_call(
        tail_kernel,
        out_shape=jax.ShapeDtypeStruct((CAP, 2, 2 * SEQ, C), BF16),
        in_specs=[vmem] * 5 + [any_space, vmem],
        out_specs=vmem,
        scratch_shapes=[
            pltpu.VMEM((3, 6 * C, 2 * C), BF16),
            pltpu.VMEM((24 * Z, 4 * C), BF16),
            pltpu.VMEM((3, 2 * CAP * SEQ, 6 * C), BF16),
            pltpu.VMEM((2 * CAP * SEQ, 2 * C), F32),
            pltpu.VMEM((CAP * SEQ, 4 * C), BF16),
            pltpu.SemaphoreType.DMA((3,)),
        ],
        compiler_params=pltpu.CompilerParams(vmem_limit_bytes=48 << 20),
    )(
        y,
        mask,
        input_kernel,
        input_bias.reshape(1, C),
        norm_gain.reshape(1, C),
        block_kernel,
        block_bias.reshape(1, C),
    )


def solution(mesh):
    placed = (
        P(None, "seq", "row"),
        P(None, None, "row"),
        P("row", None),
        P(),
        P(),
        P(),
        P(),
        P(),
        P(),
        P(),
        P(),
    )
    return jax.shard_map(
        shards,
        mesh=mesh,
        in_specs=placed,
        out_specs=P(("seq", "row"), None, None, None),
        check_vma=False,
    )
```

```python
import functools

import jax
import jax.numpy as jnp
from jax import lax
from jax.experimental import pallas as pl
from jax.experimental.pallas import tpu as pltpu
from jax.sharding import PartitionSpec as P

MESH = pl.DeviceIdType.MESH
F32 = jnp.float32
BF16 = jnp.bfloat16

D = 5120
DL = 1280
Z = 16
C = 384
CAP = 4
FRAMES = 512
REQ = 64
SEQ = 64
ROW = 4
QF = FRAMES // ROW
EPSILON = 1e-06


def iota(shape, dim):
    return lax.broadcasted_iota(jnp.int32, shape, dim)


def split_bf16(x):
    high = x.astype(BF16)
    return high, (x - high.astype(F32)).astype(BF16)


def dot(a, b):
    return lax.dot_general(a, b, (((1,), (0,)), ((), ())), preferred_element_type=F32)


def dot_nt(a, b):
    return lax.dot_general(a, b, (((1,), (1,)), ((), ())), preferred_element_type=F32)


def to_rows(column, eye):
    return jnp.sum(jnp.where(eye, column, 0.0), axis=0, keepdims=True)


def to_columns(row, eye):
    return jnp.sum(jnp.where(eye, row, 0.0), axis=1, keepdims=True)


def kernel(
    hid_hbm,
    mod_hbm,
    proj_hbm,
    bias_hbm,
    ker1_hbm,
    bias1_hbm,
    gain_hbm,
    ker2_hbm,
    bias2_hbm,
    counts_hbm,
    plan_hbm,
    out_hbm,
    hid,
    mod,
    proj,
    bias,
    counts,
    plan,
    ker1,
    bias1,
    gain,
    bias2,
    stats,
    stats_in,
    part,
    tok,
    tok_out,
    tok_in,
    spread,
    onehot,
    sendbuf,
    recv,
    y,
    mask,
    taps,
    w1,
    lhs,
    acc,
    feat,
    out,
    local_sem,
    stat_send,
    stat_recv,
    tok_send,
    tok_recv,
    out_send,
    out_recv,
    tap_sem,
    out_sem,
):
    my_seq = lax.axis_index("seq")
    my_row = lax.axis_index("row")

    loads = [
        pltpu.make_async_copy(counts_hbm, counts, local_sem.at[0]),
        pltpu.make_async_copy(plan_hbm, plan, local_sem.at[1]),
        pltpu.make_async_copy(proj_hbm, proj, local_sem.at[2]),
        pltpu.make_async_copy(mod_hbm, mod, local_sem.at[3]),
        pltpu.make_async_copy(bias_hbm, bias, local_sem.at[4]),
        pltpu.make_async_copy(ker1_hbm, ker1, local_sem.at[5]),
        pltpu.make_async_copy(bias1_hbm, bias1, local_sem.at[6]),
        pltpu.make_async_copy(gain_hbm, gain, local_sem.at[7]),
        pltpu.make_async_copy(bias2_hbm, bias2, local_sem.at[8]),
    ]
    hid_loads = [
        pltpu.make_async_copy(
            hid_hbm.at[pl.ds(QF * q, QF)], hid.at[pl.ds(QF * q, QF)], local_sem.at[9 + q]
        )
        for q in range(ROW)
    ]
    for copy in hid_loads + loads:
        copy.start()

    barrier = pltpu.get_barrier_semaphore()
    for i in range(1, ROW):
        pl.semaphore_signal(
            barrier,
            inc=1,
            device_id=(my_seq, lax.rem(my_row + i, ROW)),
            device_id_type=MESH,
        )

    def greet(i, carry):
        pl.semaphore_signal(
            barrier,
            inc=1,
            device_id=(lax.rem(my_seq + i, SEQ), my_row),
            device_id_type=MESH,
        )
        return carry

    lax.fori_loop(1, SEQ, greet, 0)

    eye = iota((QF, QF), 0) == iota((QF, QF), 1)

    for copy in loads[0:2]:
        copy.wait()
    counts_row = counts[...].astype(F32)
    square = (REQ, REQ)
    counts_col = jnp.sum(
        jnp.where(iota(square, 0) == iota(square, 1), counts_row, 0.0), axis=1, keepdims=True
    )
    ends_col = jnp.sum(
        jnp.where(iota(square, 1) <= iota(square, 0), counts_row, 0.0), axis=1, keepdims=True
    )
    starts_col = ends_col - counts_col
    wide = (REQ, 2 * REQ)
    request_lane = lax.rem(iota(wide, 1), REQ)
    ends_row = jnp.sum(
        jnp.where(iota(wide, 0) <= request_lane, counts_col, 0.0), axis=0, keepdims=True
    )
    starts_row = jnp.sum(
        jnp.where(iota(wide, 0) < request_lane, counts_col, 0.0), axis=0, keepdims=True
    )

    plan_row = plan[...]
    plan_f32 = plan_row.astype(F32)
    frame_row = iota((1, FRAMES), 1)
    frame_f32 = frame_row.astype(F32)
    rank = jnp.zeros((1, FRAMES), F32)
    for q in range(ROW):
        plan_col = to_columns(plan_f32[:, QF * q : QF * (q + 1)], eye)
        before = iota((QF, FRAMES), 0) + QF * q < iota((QF, FRAMES), 1)
        rank += jnp.sum(
            jnp.where(jnp.logical_and(plan_col == plan_f32, before), 1.0, 0.0),
            axis=0,
            keepdims=True,
        )
    code = jnp.where(
        plan_row - (plan_row // ROW) * ROW == my_row,
        (plan_row // ROW).astype(F32) * CAP + rank,
        -1.0,
    )
    by_request = (REQ, FRAMES)
    frame_of = iota(by_request, 1).astype(F32)
    first = jnp.sum(
        jnp.where(
            jnp.logical_and(frame_of >= starts_col, frame_of < ends_col), starts_col, 0.0
        ),
        axis=0,
        keepdims=True,
    )
    shifted = []
    for back in range(5):
        if back == 0:
            shifted.append(code)
            continue
        code_ahead = pltpu.roll(jnp.broadcast_to(code, (8, FRAMES)), FRAMES - back, 1)[0:1]
        first_ahead = pltpu.roll(jnp.broadcast_to(first, (8, FRAMES)), FRAMES - back, 1)[0:1]
        shifted.append(
            jnp.where(
                jnp.logical_and(first_ahead <= frame_f32, frame_row < FRAMES - back),
                code_ahead,
                -1.0,
            )
        )
    table = []
    for high in range(2):
        rows = iota((16, FRAMES), 0)
        place = lax.rem(rows, 4)
        picked = jnp.broadcast_to(shifted[1 - high], (16, FRAMES))
        for at in range(3):
            picked = jnp.where(place == at, shifted[4 - at - high], picked)
        table.append(picked - (rows // 4).astype(F32))
    table = jnp.concatenate(table, axis=1)

    means = []
    for q in range(ROW):
        hid_loads[q].wait()
        h = hid[QF * q : QF * (q + 1), :].astype(F32)
        one = jnp.sum(h, axis=1, keepdims=True)
        two = jnp.sum(h * h, axis=1, keepdims=True)
        means.append(one / DL)
        stats[q : q + 1, :] = to_rows(one, eye)
        stats[ROW + q : ROW + q + 1, :] = to_rows(two, eye)

    pl.semaphore_wait(barrier, ROW - 1 + SEQ - 1)
    stat_copies = []
    for i in range(1, ROW):
        copy = pltpu.make_async_remote_copy(
            src_ref=stats,
            dst_ref=stats_in.at[i - 1],
            send_sem=stat_send.at[i - 1],
            recv_sem=stat_recv.at[i - 1],
            device_id=(my_seq, lax.rem(my_row + i, ROW)),
            device_id_type=MESH,
        )
        copy.start()
        stat_copies.append(copy)

    for t in range(3):
        for p in range(2):
            for e in range(3):
                for i in range(2):
                    pltpu.make_async_copy(
                        ker2_hbm.at[9 * t + 3 * (p - i + 1) + e],
                        taps.at[t, pl.ds((3 * p + e) * C, C), pl.ds(i * C, C)],
                        tap_sem.at[t],
                    ).start()


    for copy in loads[2:]:
        copy.wait()

    lanes = (Z * 4, 2 * Z * 4)
    lane = lax.rem(iota(lanes, 1), 4 * Z)
    wanted = lax.rem(lane // Z, 2) * (2 * Z) + (lane // (2 * Z)) * Z + lax.rem(lane, Z)
    reorder = jnp.where(iota(lanes, 0) == wanted, 1.0, 0.0).astype(BF16)
    weight = lax.dot_general(
        proj[...], reorder, (((0,), (0,)), ((), ())), preferred_element_type=F32
    ).astype(BF16)
    bias_hi, bias_lo = split_bf16(jnp.broadcast_to(bias[...], (16, 4 * Z)))
    bias_lo2 = (
        jnp.broadcast_to(bias[...], (16, 4 * Z)) - bias_hi.astype(F32) - bias_lo.astype(F32)
    ).astype(BF16)
    bias_row = (dot(bias_hi, reorder) + dot(bias_lo, reorder) + dot(bias_lo2, reorder))[0:1, :]

    gain_hi, gain_lo = split_bf16(1.0 + mod[:, 1, :])
    shift_hi, shift_lo = split_bf16(mod[:, 0, :])
    gain_weight = dot(gain_hi, weight) + dot(gain_lo, weight)
    shift_weight = dot(shift_hi, weight) + dot(shift_lo, weight)
    gains = jnp.concatenate([gain_hi, gain_lo], axis=0)
    per_request = jnp.concatenate([gain_weight, shift_weight], axis=1)
    request_hi, request_lo = split_bf16(per_request)
    per_request = jnp.concatenate([request_hi, request_lo], axis=0)

    for q in range(ROW):
        frame = (iota((QF, 2 * REQ), 0) + QF * q).astype(F32)
        member = jnp.where(
            jnp.logical_and(frame >= starts_row, frame < ends_row), 1.0, 0.0
        ).astype(BF16)
        frame_gain = dot(member, gains)
        h = hid[QF * q : QF * (q + 1), :].astype(F32)
        x_hi, x_lo = split_bf16((h - means[q]) * frame_gain)
        part[QF * q : QF * (q + 1), 0:128] = dot(x_hi, weight) + dot(x_lo, weight)
        part[QF * q : QF * (q + 1), 128:384] = dot(member, per_request)

    for copy in stat_copies:
        copy.wait_recv()
    total = stats[...] + stats_in[0] + stats_in[1] + stats_in[2]
    average_row = total[0:ROW] / D
    inverse_row = lax.rsqrt(total[ROW : 2 * ROW] / D - average_row * average_row + EPSILON)
    half = iota((QF // 2, 128), 1) < 64
    for q in range(ROW):
        average = to_columns(average_row[q : q + 1], eye)
        inverse = to_columns(inverse_row[q : q + 1], eye)
        rows = slice(QF * q, QF * (q + 1))
        share = inverse * (
            part[rows, 0:128] + (means[q] - average) * part[rows, 128:256]
        ) + part[rows, 256:384]
        tok[q] = jnp.where(half, share[0 : QF // 2], share[QF // 2 : QF])
        tok_out[q] = tok[q].astype(BF16)
    tok_copies = []
    for i in range(1, ROW):
        copy = pltpu.make_async_remote_copy(
            src_ref=tok_out,
            dst_ref=tok_in.at[i - 1],
            send_sem=tok_send.at[i - 1],
            recv_sem=tok_recv.at[i - 1],
            device_id=(my_seq, lax.rem(my_row + i, ROW)),
            device_id_type=MESH,
        )
        copy.start()
        tok_copies.append(copy)

    own = jnp.where(table == (my_seq * CAP).astype(F32), 1.0, 0.0)
    mask[0] = jnp.broadcast_to(
        jnp.sum(own[:, 0:FRAMES], axis=1, keepdims=True), (16, 128)
    )
    mask[1] = jnp.broadcast_to(
        jnp.sum(own[:, FRAMES : 2 * FRAMES], axis=1, keepdims=True), (16, 128)
    )
    for s in range(SEQ):
        onehot[16 * s : 16 * (s + 1), :] = jnp.where(table == float(CAP * s), 1.0, 0.0).astype(
            BF16
        )
    def fill(base, a, columns):
        for n, (position, q) in enumerate(columns):
            for i in range(2):
                for r in range(2):
                    e = position - r + 1
                    if 0 <= e <= 2:
                        block = ker1[9 * a + 3 * (q - i + 1) + e]
                    else:
                        block = jnp.zeros((Z, C), BF16)
                    w1[base + Z * n : base + Z * (n + 1), (2 * i + r) * C : (2 * i + r + 1) * C] = (
                        block
                    )

    own = [(0, 0), (0, 1), (1, 0), (1, 1)]
    rim = [(2, 0), (2, 1), (-1, 0), (-1, 1)]
    for base, a, columns in (
        (0, 0, own),
        (64, 1, own),
        (128, 0, rim),
        (192, 2, own),
        (256, 1, rim),
        (320, 2, rim),
    ):
        fill(base, a, columns)

    moved = (256, 256)
    to_row, from_row = iota(moved, 0), iota(moved, 1)
    group = to_row // 16
    source = lax.rem(to_row, 16) * 16 + lax.rem(group, 4) * 4 + group // 4
    mover = jnp.where(from_row == source, 1.0, 0.0).astype(BF16)

    mixed = (2 * SEQ, 2 * SEQ)
    to_row, from_row = iota(mixed, 0), iota(mixed, 1)
    mixer = jnp.where(from_row == lax.rem(to_row, 2) * SEQ + to_row // 2, 1.0, 0.0).astype(BF16)
    bias1_row = bias1[...].reshape(1, C)
    gain_row = gain[...].reshape(1, C)
    for copy in tok_copies:
        copy.wait_recv()

    for q in range(ROW):
        here = (
            (
                tok[q]
                + tok_in[0, q].astype(F32)
                + tok_in[1, q].astype(F32)
                + tok_in[2, q].astype(F32)
                + bias_row
            )
            .astype(BF16)
            .astype(F32)
        )
        there = pltpu.roll(here, 64, 1)
        low, high = jnp.where(half, here, 0.0), jnp.where(half, 0.0, here)
        low_moved, high_moved = jnp.where(half, there, 0.0), jnp.where(half, 0.0, there)
        for at, block in (
            (QF * q, low),
            (QF * q + 64, low_moved),
            (FRAMES + QF * q, high_moved),
            (FRAMES + QF * q + 64, high),
        ):
            spread[at : at + 64, :] = block.astype(BF16)
    for block in range(4):
        rows = slice(256 * block, 256 * (block + 1))
        sendbuf[16 * block : 16 * (block + 1)] = (
            dot(onehot[rows, :], spread[...]).astype(BF16).reshape(16, 16, 128)
        )

    my_y, my_z, my_core = my_seq // 16, lax.rem(my_seq, 16) // 2, lax.rem(my_seq, 2)

    def swing(j, half_way):
        step = (j + 1) // 2
        return half_way + step * (2 * lax.rem(j, 2) - 1)

    def post(i, carry):
        to_z = lax.rem(my_z + swing(i // 8, 4), 8)
        to_y = lax.rem(my_y + swing(lax.rem(i, 8) // 2, 2), 4)
        to_core = lax.rem(my_core + 1 - lax.rem(i, 2), 2)
        to = to_y * 16 + to_z * 2 + to_core
        pltpu.make_async_remote_copy(
            src_ref=sendbuf.at[to],
            dst_ref=recv.at[my_seq],
            send_sem=out_send,
            recv_sem=out_recv,
            device_id=(to, my_row),
            device_id_type=MESH,
        ).start()
        return carry

    lax.fori_loop(0, SEQ - 1, post, 0)
    recv[my_seq] = sendbuf[my_seq]

    arrived = recv.at[pl.ds(0, SEQ - 1)]
    pltpu.make_async_copy(arrived, arrived, out_recv).wait()
    for block in range(4):
        got = recv[16 * block : 16 * (block + 1)].reshape(256, 128)
        y[:, 16 * block : 16 * (block + 1), :] = (
            dot(mover, got).astype(BF16).reshape(16, 16, 128)
        )

    rows = CAP * SEQ
    column = lax.rem(iota((rows, 128), 0), SEQ)
    lane = iota((rows, 128), 1)

    def rims(v):
        right = jnp.where(column == SEQ - 1, 0.0, pltpu.roll(v, rows - 1, 0))
        left = jnp.where(column == 0, 0.0, pltpu.roll(v, 1, 0))
        return jnp.where(lax.rem(lane, 64) < 32, right, left)

    wide = [y[CAP * t : CAP * (t + 1)].reshape(rows, 128).astype(F32) for t in range(4)]
    around = [rims(v) for v in wide]
    first_col = lax.rem(iota((rows, C), 0), SEQ) == 0
    last_col = lax.rem(iota((rows, C), 0), SEQ) == SEQ - 1
    first_col = iota((SEQ, C), 0) == 0
    last_col = iota((SEQ, C), 0) == SEQ - 1
    xs = []
    for t in range(3):
        xs.append(
            jnp.concatenate(
                [wide[t], jnp.where(lane < 64, around[t], wide[t + 1]), around[t + 1]], axis=1
            ).astype(BF16)
        )

    def features(t):
        for p in range(2):
            cols = slice(2 * p * C, 2 * (p + 1) * C)
            feat[t, :, cols] = dot(xs[t], w1[:, cols])

    def activate(t):
        which, row = ((0, 2), (0, 3), (1, 3))[t]
        for k in range(CAP):
            live = 0.5 * mask[which, 4 * k + row : 4 * k + row + 1, 0:1]
            here = slice(k * SEQ, (k + 1) * SEQ)
            for p in range(2):
                for r in range(2):
                    v = feat[t, here, (2 * p + r) * C : (2 * p + r + 1) * C] + bias1_row
                    scale = lax.rsqrt(jnp.mean(v * v, axis=1, keepdims=True) + EPSILON) * live
                    n = v * scale * gain_row
                    a = n + n * jnp.tanh(n)

                    def put(side, e, value):
                        lhs[
                            t,
                            side * rows + k * SEQ : side * rows + (k + 1) * SEQ,
                            (3 * p + e) * C : (3 * p + e + 1) * C,
                        ] = value.astype(BF16)

                    if r == 0:
                        put(0, 1, a)
                        put(1, 0, a)
                        put(1, 2, jnp.where(last_col, 0.0, pltpu.roll(a, SEQ - 1, 0)))
                    else:
                        put(0, 2, a)
                        put(1, 1, a)
                        put(0, 0, jnp.where(first_col, 0.0, pltpu.roll(a, 1, 0)))

    def convolve(t):
        product = dot(lhs[t], taps[t])
        if t == 0:
            acc[...] = product
        else:
            acc[...] += product

    for t in range(3):
        features(t)
    activate(0)
    for t in range(3):
        pltpu.make_async_copy(taps.at[t], taps.at[t], tap_sem.at[t]).wait()
        convolve(t)
        if t < 2:
            activate(t + 1)

    both_bias = bias2[...].reshape(1, C) + bias1_row
    for k in range(CAP):
        live = mask[1, 4 * k + 3 : 4 * k + 4, 0:1]
        for i in range(2):
            halves = []
            for r in range(2):
                at = r * rows + k * SEQ
                halves.append(
                    (
                        (
                            feat[2, k * SEQ : (k + 1) * SEQ, (2 * i + r) * C : (2 * i + r + 1) * C]
                            + both_bias
                            + acc[at : at + SEQ, i * C : (i + 1) * C]
                        )
                        * live
                    ).astype(BF16)
                )
            out[k, i] = dot(mixer, jnp.concatenate(halves, axis=0)).astype(BF16)
        pltpu.make_async_copy(out.at[k], out_hbm.at[k], out_sem.at[k]).start()
    for k in range(CAP):
        pltpu.make_async_copy(out.at[k], out_hbm.at[k], out_sem.at[k]).wait()

    for copy in stat_copies + tok_copies:
        copy.wait_send()
    sent = sendbuf.at[pl.ds(0, SEQ - 1)]
    pltpu.make_async_copy(sent, sent, out_send).wait()


def shards(
    hidden,
    modulation,
    projection,
    projection_bias,
    input_kernel,
    input_bias,
    norm_gain,
    block_kernel,
    block_bias,
    frame_counts,
    decoder_plan,
):
    hbm = pl.BlockSpec(memory_space=pltpu.HBM)
    return pl.pallas_call(
        kernel,
        out_shape=jax.ShapeDtypeStruct((CAP, 2, 2 * SEQ, C), BF16),
        in_specs=[hbm] * 11,
        out_specs=hbm,
        scratch_shapes=[
            pltpu.VMEM((FRAMES, DL), BF16),
            pltpu.VMEM((REQ, 2, DL), F32),
            pltpu.VMEM((4 * Z, DL), BF16),
            pltpu.VMEM((1, 4 * Z), F32),
            pltpu.VMEM((1, REQ), jnp.int32),
            pltpu.VMEM((1, FRAMES), jnp.int32),
            pltpu.VMEM((27, Z, C), BF16),
            pltpu.VMEM((C,), F32),
            pltpu.VMEM((C,), F32),
            pltpu.VMEM((C,), F32),
            pltpu.VMEM((2 * ROW, QF), F32),
            pltpu.VMEM((ROW - 1, 2 * ROW, QF), F32),
            pltpu.VMEM((FRAMES, 384), F32),
            pltpu.VMEM((ROW, QF // 2, 128), F32),
            pltpu.VMEM((ROW, QF // 2, 128), BF16),
            pltpu.VMEM((ROW - 1, ROW, QF // 2, 128), BF16),
            pltpu.VMEM((2 * FRAMES, 128), BF16),
            pltpu.VMEM((16 * SEQ, 2 * FRAMES), BF16),
            pltpu.VMEM((SEQ, 16, 128), BF16),
            pltpu.VMEM((SEQ, 16, 128), BF16),
            pltpu.VMEM((16, SEQ, 128), BF16),
            pltpu.VMEM((2, 16, 128), F32),
            pltpu.VMEM((3, 6 * C, 2 * C), BF16),
            pltpu.VMEM((24 * Z, 4 * C), BF16),
            pltpu.VMEM((3, 2 * CAP * SEQ, 6 * C), BF16),
            pltpu.VMEM((2 * CAP * SEQ, 2 * C), F32),
            pltpu.VMEM((3, CAP * SEQ, 4 * C), F32),
            pltpu.VMEM((CAP, 2, 2 * SEQ, C), BF16),
            pltpu.SemaphoreType.DMA((9 + ROW,)),
            pltpu.SemaphoreType.DMA((ROW - 1,)),
            pltpu.SemaphoreType.DMA((ROW - 1,)),
            pltpu.SemaphoreType.DMA((ROW - 1,)),
            pltpu.SemaphoreType.DMA((ROW - 1,)),
            pltpu.SemaphoreType.DMA,
            pltpu.SemaphoreType.DMA,
            pltpu.SemaphoreType.DMA((3,)),
            pltpu.SemaphoreType.DMA((CAP,)),
        ],
        compiler_params=pltpu.CompilerParams(
            collective_id=0, has_side_effects=True, vmem_limit_bytes=56 << 20
        ),
    )(
        hidden.reshape(FRAMES, DL),
        modulation,
        projection.T,
        projection_bias.reshape(1, 4 * Z),
        input_kernel,
        input_bias,
        norm_gain,
        block_kernel,
        block_bias,
        frame_counts.reshape(1, REQ),
        decoder_plan.reshape(1, FRAMES),
    )


def solution(mesh):
    placed = (
        P(None, "seq", "row"),
        P(None, None, "row"),
        P("row", None),
        P(),
        P(),
        P(),
        P(),
        P(),
        P(),
        P(),
        P(),
    )
    return jax.shard_map(
        shards,
        mesh=mesh,
        in_specs=placed,
        out_specs=P(("seq", "row"), None, None, None),
        check_vma=False,
    )
```

```python
import functools

import jax
import jax.numpy as jnp
from jax import lax
from jax.experimental import pallas as pl
from jax.experimental.pallas import tpu as pltpu
from jax.sharding import PartitionSpec as P

MESH = pl.DeviceIdType.MESH
F32 = jnp.float32
BF16 = jnp.bfloat16

D = 5120
DL = 1280
Z = 16
C = 384
CAP = 4
FRAMES = 512
REQ = 64
SEQ = 64
ROW = 4
QF = FRAMES // ROW
EPSILON = 1e-06


def iota(shape, dim):
    return lax.broadcasted_iota(jnp.int32, shape, dim)


def split_bf16(x):
    high = x.astype(BF16)
    return high, (x - high.astype(F32)).astype(BF16)


def dot(a, b):
    return lax.dot_general(a, b, (((1,), (0,)), ((), ())), preferred_element_type=F32)


def dot_nt(a, b):
    return lax.dot_general(a, b, (((1,), (1,)), ((), ())), preferred_element_type=F32)


def to_rows(column, eye):
    return jnp.sum(jnp.where(eye, column, 0.0), axis=0, keepdims=True)


def to_columns(row, eye):
    return jnp.sum(jnp.where(eye, row, 0.0), axis=1, keepdims=True)


def kernel(
    hid_hbm,
    mod_hbm,
    proj_hbm,
    bias_hbm,
    ker1_hbm,
    bias1_hbm,
    gain_hbm,
    ker2_hbm,
    bias2_hbm,
    counts_hbm,
    plan_hbm,
    out,
    hid,
    mod,
    proj,
    bias,
    counts,
    plan,
    ker1,
    bias1,
    gain,
    bias2,
    stats,
    stats_in,
    weight,
    gains,
    share,
    share_in,
    base,
    scale,
    tok,
    tok_out,
    tok_in,
    spread,
    onehot,
    sendbuf,
    recv,
    y,
    mask,
    taps,
    w1,
    lhs,
    acc,
    feat,
    mix,
    local_sem,
    stat_send,
    stat_recv,
    share_send,
    share_recv,
    tok_send,
    tok_recv,
    out_send,
    out_recv,
    tap_sem,
):
    my_seq = lax.axis_index("seq")
    my_row = lax.axis_index("row")

    loads = [
        pltpu.make_async_copy(counts_hbm, counts, local_sem.at[0]),
        pltpu.make_async_copy(plan_hbm, plan, local_sem.at[1]),
        pltpu.make_async_copy(proj_hbm, proj, local_sem.at[2]),
        pltpu.make_async_copy(mod_hbm, mod, local_sem.at[3]),
        pltpu.make_async_copy(bias_hbm, bias, local_sem.at[4]),
        pltpu.make_async_copy(ker1_hbm, ker1, local_sem.at[5]),
        pltpu.make_async_copy(bias1_hbm, bias1, local_sem.at[6]),
        pltpu.make_async_copy(gain_hbm, gain, local_sem.at[7]),
        pltpu.make_async_copy(bias2_hbm, bias2, local_sem.at[8]),
    ]
    hid_loads = [
        pltpu.make_async_copy(
            hid_hbm.at[pl.ds(QF * q, QF)], hid.at[pl.ds(QF * q, QF)], local_sem.at[9 + q]
        )
        for q in range(ROW)
    ]
    for copy in hid_loads + loads:
        copy.start()

    barrier = pltpu.get_barrier_semaphore()
    for i in range(1, ROW):
        pl.semaphore_signal(
            barrier,
            inc=1,
            device_id=(my_seq, lax.rem(my_row + i, ROW)),
            device_id_type=MESH,
        )

    def greet(i, carry):
        pl.semaphore_signal(
            barrier,
            inc=1,
            device_id=(lax.rem(my_seq + i, SEQ), my_row),
            device_id_type=MESH,
        )
        return carry

    lax.fori_loop(1, SEQ, greet, 0)

    eye = iota((QF, QF), 0) == iota((QF, QF), 1)

    for copy in loads[0:2]:
        copy.wait()
    counts_row = counts[...].astype(F32)
    square = (REQ, REQ)
    counts_col = jnp.sum(
        jnp.where(iota(square, 0) == iota(square, 1), counts_row, 0.0), axis=1, keepdims=True
    )
    ends_col = jnp.sum(
        jnp.where(iota(square, 1) <= iota(square, 0), counts_row, 0.0), axis=1, keepdims=True
    )
    starts_col = ends_col - counts_col
    wide = (REQ, 2 * REQ)
    request_lane = lax.rem(iota(wide, 1), REQ)
    ends_row = jnp.sum(
        jnp.where(iota(wide, 0) <= request_lane, counts_col, 0.0), axis=0, keepdims=True
    )
    starts_row = jnp.sum(
        jnp.where(iota(wide, 0) < request_lane, counts_col, 0.0), axis=0, keepdims=True
    )

    plan_row = plan[...]
    plan_f32 = plan_row.astype(F32)
    frame_row = iota((1, FRAMES), 1)
    frame_f32 = frame_row.astype(F32)
    rank = jnp.zeros((1, FRAMES), F32)
    for q in range(ROW):
        plan_col = to_columns(plan_f32[:, QF * q : QF * (q + 1)], eye)
        before = iota((QF, FRAMES), 0) + QF * q < iota((QF, FRAMES), 1)
        rank += jnp.sum(
            jnp.where(jnp.logical_and(plan_col == plan_f32, before), 1.0, 0.0),
            axis=0,
            keepdims=True,
        )
    code = jnp.where(
        plan_row - (plan_row // ROW) * ROW == my_row,
        (plan_row // ROW).astype(F32) * CAP + rank,
        -1.0,
    )
    by_request = (REQ, FRAMES)
    frame_of = iota(by_request, 1).astype(F32)
    first = jnp.sum(
        jnp.where(
            jnp.logical_and(frame_of >= starts_col, frame_of < ends_col), starts_col, 0.0
        ),
        axis=0,
        keepdims=True,
    )
    shifted = []
    for back in range(5):
        if back == 0:
            shifted.append(code)
            continue
        code_ahead = pltpu.roll(jnp.broadcast_to(code, (8, FRAMES)), FRAMES - back, 1)[0:1]
        first_ahead = pltpu.roll(jnp.broadcast_to(first, (8, FRAMES)), FRAMES - back, 1)[0:1]
        shifted.append(
            jnp.where(
                jnp.logical_and(first_ahead <= frame_f32, frame_row < FRAMES - back),
                code_ahead,
                -1.0,
            )
        )
    table = []
    for high in range(2):
        rows = iota((16, FRAMES), 0)
        place = lax.rem(rows, 4)
        picked = jnp.broadcast_to(shifted[1 - high], (16, FRAMES))
        for at in range(3):
            picked = jnp.where(place == at, shifted[4 - at - high], picked)
        table.append(picked - (rows // 4).astype(F32))
    table = jnp.concatenate(table, axis=1)

    for copy in loads[2:5]:
        copy.wait()

    lanes = (Z * 4, 2 * Z * 4)
    lane = lax.rem(iota(lanes, 1), 4 * Z)
    wanted = lax.rem(lane // Z, 2) * (2 * Z) + (lane // (2 * Z)) * Z + lax.rem(lane, Z)
    reorder = jnp.where(iota(lanes, 0) == wanted, 1.0, 0.0).astype(BF16)
    weight[...] = lax.dot_general(
        proj[...], reorder, (((0,), (0,)), ((), ())), preferred_element_type=F32
    ).astype(BF16)
    bias_hi, bias_lo = split_bf16(jnp.broadcast_to(bias[...], (16, 4 * Z)))
    bias_lo2 = (
        jnp.broadcast_to(bias[...], (16, 4 * Z)) - bias_hi.astype(F32) - bias_lo.astype(F32)
    ).astype(BF16)
    bias_row = (dot(bias_hi, reorder) + dot(bias_lo, reorder) + dot(bias_lo2, reorder))[0:1, :]

    gain_hi, gain_lo = split_bf16(1.0 + mod[:, 1, :])
    shift_hi, shift_lo = split_bf16(mod[:, 0, :])
    gain_weight = dot(gain_hi, weight[...]) + dot(gain_lo, weight[...])
    shift_weight = dot(shift_hi, weight[...]) + dot(shift_lo, weight[...])
    gains[0:REQ, :] = gain_hi
    gains[REQ : 2 * REQ, :] = gain_lo
    share[...] = jnp.where(iota((REQ, 128), 1) < 64, gain_weight, shift_weight)

    members = []
    for q in range(ROW):
        frame = (iota((QF, 2 * REQ), 0) + QF * q).astype(F32)
        members.append(
            jnp.where(
                jnp.logical_and(frame >= starts_row, frame < ends_row), 1.0, 0.0
            ).astype(BF16)
        )

    pl.semaphore_wait(barrier, ROW - 1 + SEQ - 1)
    share_copies, stat_copies, tok_copies = [], [], []
    for i in range(1, ROW):
        copy = pltpu.make_async_remote_copy(
            src_ref=share,
            dst_ref=share_in.at[i - 1],
            send_sem=share_send.at[i - 1],
            recv_sem=share_recv.at[i - 1],
            device_id=(my_seq, lax.rem(my_row + i, ROW)),
            device_id_type=MESH,
        )
        copy.start()
        share_copies.append(copy)

    half = iota((QF // 2, 128), 1) < 64
    share_rows = jnp.concatenate(split_bf16(gain_weight), axis=0)
    means = []
    for q in range(ROW):
        hid_loads[q].wait()
        rows = slice(QF * q, QF * (q + 1))
        one = two = projected = jnp.zeros((QF, 128), F32)
        for c in range(DL // 256):
            cols = slice(256 * c, 256 * (c + 1))
            h = hid[rows, cols].astype(F32)
            square_h = h * h
            one += h[:, 0:128] + h[:, 128:256]
            two += square_h[:, 0:128] + square_h[:, 128:256]
            x_hi, x_lo = split_bf16(h * dot(members[q], gains[:, cols]))
            projected += dot(x_hi, weight[cols, :]) + dot(x_lo, weight[cols, :])
        one = jnp.sum(one, axis=1, keepdims=True)
        two = jnp.sum(two, axis=1, keepdims=True)
        means.append(one / DL)
        stats[q : q + 1, :] = to_rows(one, eye)
        stats[ROW + q : ROW + q + 1, :] = to_rows(two, eye)
        projected = projected - means[q] * dot(members[q], share_rows)
        tok[q] = jnp.where(half, projected[0 : QF // 2], projected[QF // 2 : QF])
        tok_out[q] = tok[q].astype(BF16)
        for i in range(1, ROW):
            copy = pltpu.make_async_remote_copy(
                src_ref=tok_out.at[q],
                dst_ref=tok_in.at[i - 1, q],
                send_sem=tok_send.at[q, i - 1],
                recv_sem=tok_recv.at[q, i - 1],
                device_id=(my_seq, lax.rem(my_row + i, ROW)),
                device_id_type=MESH,
            )
            copy.start()
            tok_copies.append(copy)
    for i in range(1, ROW):
        copy = pltpu.make_async_remote_copy(
            src_ref=stats,
            dst_ref=stats_in.at[i - 1],
            send_sem=stat_send.at[i - 1],
            recv_sem=stat_recv.at[i - 1],
            device_id=(my_seq, lax.rem(my_row + i, ROW)),
            device_id_type=MESH,
        )
        copy.start()
        stat_copies.append(copy)

    for t in range(3):
        for p in range(2):
            for e in range(3):
                for i in range(2):
                    pltpu.make_async_copy(
                        ker2_hbm.at[9 * t + 3 * (p - i + 1) + e],
                        taps.at[t, pl.ds((3 * p + e) * C, C), pl.ds(i * C, C)],
                        tap_sem.at[t],
                    ).start()


    own = jnp.where(table == (my_seq * CAP).astype(F32), 1.0, 0.0)
    mask[0] = jnp.broadcast_to(
        jnp.sum(own[:, 0:FRAMES], axis=1, keepdims=True), (16, 128)
    )
    mask[1] = jnp.broadcast_to(
        jnp.sum(own[:, FRAMES : 2 * FRAMES], axis=1, keepdims=True), (16, 128)
    )
    for s in range(SEQ):
        onehot[16 * s : 16 * (s + 1), :] = jnp.where(table == float(CAP * s), 1.0, 0.0).astype(
            BF16
        )

    for copy in share_copies + stat_copies:
        copy.wait_recv()
    total = stats[...] + stats_in[0] + stats_in[1] + stats_in[2]
    average_row = total[0:ROW] / D
    inverse_row = lax.rsqrt(total[ROW : 2 * ROW] / D - average_row * average_row + EPSILON)
    shares = [share[...], share_in[0], share_in[1], share_in[2]]
    left_half = iota((REQ, 128), 1) < 64
    shift_total = shares[0] + shares[1] + shares[2] + shares[3]
    spreads = [jnp.where(left_half, v, pltpu.roll(v, 64, 1)) for v in shares]
    spreads.append(jnp.where(left_half, pltpu.roll(shift_total, 64, 1), shift_total))
    spreads = jnp.concatenate(split_bf16(jnp.concatenate(spreads, axis=1)), axis=0)
    sums = [stats, stats_in.at[0], stats_in.at[1], stats_in.at[2]]
    for q in range(ROW):
        by_frame = dot(members[q], spreads)
        inverse = to_columns(inverse_row[q : q + 1], eye)
        rest = by_frame[:, 512:640] + bias_row
        for n in range(ROW):
            offset = (sums[n][q : q + 1, :] / DL - average_row[q : q + 1]) * inverse_row[q : q + 1]
            rest += to_columns(offset, eye) * by_frame[:, 128 * n : 128 * (n + 1)]
        base[q] = jnp.where(half, rest[0 : QF // 2], rest[QF // 2 : QF])
        scale[q] = jnp.where(half, inverse[0 : QF // 2], inverse[QF // 2 : QF])

    for copy in loads[5:]:
        copy.wait()

    def fill(start, a, columns):
        for n, (position, q) in enumerate(columns):
            for i in range(2):
                for r in range(2):
                    e = position - r + 1
                    if 0 <= e <= 2:
                        block = ker1[9 * a + 3 * (q - i + 1) + e]
                    else:
                        block = jnp.zeros((Z, C), BF16)
                    w1[start + Z * n : start + Z * (n + 1), (2 * i + r) * C : (2 * i + r + 1) * C] = (
                        block
                    )

    own = [(0, 0), (0, 1), (1, 0), (1, 1)]
    rim = [(2, 0), (2, 1), (-1, 0), (-1, 1)]
    for start, a, columns in (
        (0, 0, own),
        (64, 1, own),
        (128, 0, rim),
        (192, 2, own),
        (256, 1, rim),
        (320, 2, rim),
    ):
        fill(start, a, columns)

    moved = (256, 256)
    to_row, from_row = iota(moved, 0), iota(moved, 1)
    group = to_row // 16
    source = lax.rem(to_row, 16) * 16 + lax.rem(group, 4) * 4 + group // 4
    mover = jnp.where(from_row == source, 1.0, 0.0).astype(BF16)

    bias1_row = bias1[...].reshape(1, C)
    gain_row = gain[...].reshape(1, C)

    for q in range(ROW):
        for copy in tok_copies[(ROW - 1) * q : (ROW - 1) * (q + 1)]:
            copy.wait_recv()
        here = (
            (
                (
                    tok[q]
                    + tok_in[0, q].astype(F32)
                    + tok_in[1, q].astype(F32)
                    + tok_in[2, q].astype(F32)
                )
                * scale[q]
                + base[q]
            )
            .astype(BF16)
            .astype(F32)
        )
        there = pltpu.roll(here, 64, 1)
        low, high = jnp.where(half, here, 0.0), jnp.where(half, 0.0, here)
        low_moved, high_moved = jnp.where(half, there, 0.0), jnp.where(half, 0.0, there)
        for at, block in (
            (QF * q, low),
            (QF * q + 64, low_moved),
            (FRAMES + QF * q, high_moved),
            (FRAMES + QF * q + 64, high),
        ):
            spread[at : at + 64, :] = block.astype(BF16)
    for block in range(4):
        rows = slice(256 * block, 256 * (block + 1))
        sendbuf[16 * block : 16 * (block + 1)] = (
            dot(onehot[rows, :], spread[...]).astype(BF16).reshape(16, 16, 128)
        )

    my_y, my_z, my_core = my_seq // 16, lax.rem(my_seq, 16) // 2, lax.rem(my_seq, 2)

    def swing(j, half_way):
        step = (j + 1) // 2
        return half_way + step * (2 * lax.rem(j, 2) - 1)

    def post(i, carry):
        to_z = lax.rem(my_z + swing(i // 8, 4), 8)
        to_y = lax.rem(my_y + swing(lax.rem(i, 8) // 2, 2), 4)
        to_core = lax.rem(my_core + 1 - lax.rem(i, 2), 2)
        to = to_y * 16 + to_z * 2 + to_core
        pltpu.make_async_remote_copy(
            src_ref=sendbuf.at[to],
            dst_ref=recv.at[my_seq],
            send_sem=out_send,
            recv_sem=out_recv,
            device_id=(to, my_row),
            device_id_type=MESH,
        ).start()
        return carry

    lax.fori_loop(0, SEQ - 1, post, 0)
    recv[my_seq] = sendbuf[my_seq]

    for t in range(3):
        pltpu.make_async_copy(taps.at[t], taps.at[t], tap_sem.at[t]).wait()
    arrived = recv.at[pl.ds(0, SEQ - 1)]
    pltpu.make_async_copy(arrived, arrived, out_recv).wait()
    for block in range(4):
        got = recv[16 * block : 16 * (block + 1)].reshape(256, 128)
        y[:, 16 * block : 16 * (block + 1), :] = (
            dot(mover, got).astype(BF16).reshape(16, 16, 128)
        )

    rows = CAP * SEQ
    column = lax.rem(iota((rows, 128), 0), SEQ)
    lane = iota((rows, 128), 1)

    def rims(v):
        right = jnp.where(column == SEQ - 1, 0.0, pltpu.roll(v, rows - 1, 0))
        left = jnp.where(column == 0, 0.0, pltpu.roll(v, 1, 0))
        return jnp.where(lax.rem(lane, 64) < 32, right, left)

    wide = [y[CAP * t : CAP * (t + 1)].reshape(rows, 128).astype(F32) for t in range(4)]
    around = [rims(v) for v in wide]
    first_col = iota((SEQ, C), 0) == 0
    last_col = iota((SEQ, C), 0) == SEQ - 1
    xs = []
    for t in range(3):
        xs.append(
            jnp.concatenate(
                [wide[t], jnp.where(lane < 64, around[t], wide[t + 1]), around[t + 1]], axis=1
            ).astype(BF16)
        )

    def features(t):
        for p in range(2):
            cols = slice(2 * p * C, 2 * (p + 1) * C)
            feat[t, :, cols] = dot(xs[t], w1[:, cols])

    def activate(t):
        which, row = ((0, 2), (0, 3), (1, 3))[t]
        for k in range(CAP):
            live = 0.5 * mask[which, 4 * k + row : 4 * k + row + 1, 0:1]
            here = slice(k * SEQ, (k + 1) * SEQ)
            for p in range(2):
                for r in range(2):
                    v = feat[t, here, (2 * p + r) * C : (2 * p + r + 1) * C] + bias1_row
                    factor = lax.rsqrt(jnp.mean(v * v, axis=1, keepdims=True) + EPSILON) * live
                    n = v * factor * gain_row
                    a = n + n * jnp.tanh(n)

                    def put(side, e, value):
                        lhs[
                            t,
                            side * rows + k * SEQ : side * rows + (k + 1) * SEQ,
                            (3 * p + e) * C : (3 * p + e + 1) * C,
                        ] = value.astype(BF16)

                    if r == 0:
                        put(0, 1, a)
                        put(1, 0, a)
                        put(1, 2, jnp.where(last_col, 0.0, pltpu.roll(a, SEQ - 1, 0)))
                    else:
                        put(0, 2, a)
                        put(1, 1, a)
                        put(0, 0, jnp.where(first_col, 0.0, pltpu.roll(a, 1, 0)))

    features(0)
    activate(0)
    for t in range(2):
        features(t + 1)
        product = dot(lhs[t], taps[t])
        if t == 0:
            acc[...] = product
        else:
            acc[...] += product
        activate(t + 1)

    both_bias = bias2[...].reshape(1, C) + bias1_row
    for n in range(3):
        product = dot(lhs[2], taps[2, :, 256 * n : 256 * (n + 1)])
        for part in range(2):
            at = 2 * n + part
            i, at_c = at // 3, 128 * (at % 3)
            for k in range(CAP):
                live = mask[1, 4 * k + 3 : 4 * k + 4, 0:1]
                for r in range(2):
                    here = slice(r * rows + k * SEQ, r * rows + (k + 1) * SEQ)
                    col = (2 * i + r) * C + at_c
                    mix[part, k, pl.ds(r, SEQ, stride=2), :] = (
                        product[here, 128 * part : 128 * (part + 1)]
                        + acc[here, 128 * at : 128 * (at + 1)]
                        + feat[2, k * SEQ : (k + 1) * SEQ, col : col + 128]
                        + both_bias[:, at_c : at_c + 128]
                    ) * live
                out[k, i, :, at_c : at_c + 128] = mix[part, k].astype(BF16)

    for copy in share_copies + stat_copies + tok_copies:
        copy.wait_send()
    sent = sendbuf.at[pl.ds(0, SEQ - 1)]
    pltpu.make_async_copy(sent, sent, out_send).wait()


def shards(
    hidden,
    modulation,
    projection,
    projection_bias,
    input_kernel,
    input_bias,
    norm_gain,
    block_kernel,
    block_bias,
    frame_counts,
    decoder_plan,
):
    hbm = pl.BlockSpec(memory_space=pltpu.HBM)
    return pl.pallas_call(
        kernel,
        out_shape=jax.ShapeDtypeStruct((CAP, 2, 2 * SEQ, C), BF16),
        in_specs=[hbm] * 11,
        out_specs=pl.BlockSpec(memory_space=pltpu.VMEM),
        scratch_shapes=[
            pltpu.VMEM((FRAMES, DL), BF16),
            pltpu.VMEM((REQ, 2, DL), F32),
            pltpu.VMEM((4 * Z, DL), BF16),
            pltpu.VMEM((1, 4 * Z), F32),
            pltpu.VMEM((1, REQ), jnp.int32),
            pltpu.VMEM((1, FRAMES), jnp.int32),
            pltpu.VMEM((27, Z, C), BF16),
            pltpu.VMEM((C,), F32),
            pltpu.VMEM((C,), F32),
            pltpu.VMEM((C,), F32),
            pltpu.VMEM((2 * ROW, QF), F32),
            pltpu.VMEM((ROW - 1, 2 * ROW, QF), F32),
            pltpu.VMEM((DL, 128), BF16),
            pltpu.VMEM((2 * REQ, DL), BF16),
            pltpu.VMEM((REQ, 128), F32),
            pltpu.VMEM((ROW - 1, REQ, 128), F32),
            pltpu.VMEM((ROW, QF // 2, 128), F32),
            pltpu.VMEM((ROW, QF // 2, 128), F32),
            pltpu.VMEM((ROW, QF // 2, 128), F32),
            pltpu.VMEM((ROW, QF // 2, 128), BF16),
            pltpu.VMEM((ROW - 1, ROW, QF // 2, 128), BF16),
            pltpu.VMEM((2 * FRAMES, 128), BF16),
            pltpu.VMEM((16 * SEQ, 2 * FRAMES), BF16),
            pltpu.VMEM((SEQ, 16, 128), BF16),
            pltpu.VMEM((SEQ, 16, 128), BF16),
            pltpu.VMEM((16, SEQ, 128), BF16),
            pltpu.VMEM((2, 16, 128), F32),
            pltpu.VMEM((3, 6 * C, 2 * C), BF16),
            pltpu.VMEM((24 * Z, 4 * C), BF16),
            pltpu.VMEM((3, 2 * CAP * SEQ, 6 * C), BF16),
            pltpu.VMEM((2 * CAP * SEQ, 2 * C), F32),
            pltpu.VMEM((3, CAP * SEQ, 4 * C), F32),
            pltpu.VMEM((2, CAP, 2 * SEQ, 128), F32),
            pltpu.SemaphoreType.DMA((9 + ROW,)),
            pltpu.SemaphoreType.DMA((ROW - 1,)),
            pltpu.SemaphoreType.DMA((ROW - 1,)),
            pltpu.SemaphoreType.DMA((ROW - 1,)),
            pltpu.SemaphoreType.DMA((ROW - 1,)),
            pltpu.SemaphoreType.DMA((ROW, ROW - 1)),
            pltpu.SemaphoreType.DMA((ROW, ROW - 1)),
            pltpu.SemaphoreType.DMA,
            pltpu.SemaphoreType.DMA,
            pltpu.SemaphoreType.DMA((3,)),
        ],
        compiler_params=pltpu.CompilerParams(
            collective_id=0, has_side_effects=True, vmem_limit_bytes=44 << 20
        ),
    )(*[pltpu.with_memory_space_constraint(x, pltpu.HBM) for x in (
        hidden.reshape(FRAMES, DL),
        modulation,
        projection.T,
        projection_bias.reshape(1, 4 * Z),
        input_kernel,
        input_bias,
        norm_gain,
        block_kernel,
        block_bias,
        frame_counts.reshape(1, REQ),
        decoder_plan.reshape(1, FRAMES),
    )])


def solution(mesh):
    placed = (
        P(None, "seq", "row"),
        P(None, None, "row"),
        P("row", None),
        P(),
        P(),
        P(),
        P(),
        P(),
        P(),
        P(),
        P(),
    )
    return jax.shard_map(
        shards,
        mesh=mesh,
        in_specs=placed,
        out_specs=P(("seq", "row"), None, None, None),
        check_vma=False,
    )
```

```python
import functools

import jax
import jax.numpy as jnp
from jax import lax
from jax.experimental import pallas as pl
from jax.experimental.pallas import tpu as pltpu
from jax.sharding import PartitionSpec as P

MESH = pl.DeviceIdType.MESH
F32 = jnp.float32
BF16 = jnp.bfloat16

D = 5120
DL = 1280
Z = 16
C = 384
CAP = 4
FRAMES = 512
REQ = 64
SEQ = 64
ROW = 4
QF = FRAMES // ROW
EPSILON = 1e-06


def iota(shape, dim):
    return lax.broadcasted_iota(jnp.int32, shape, dim)


def split_bf16(x):
    high = x.astype(BF16)
    return high, (x - high.astype(F32)).astype(BF16)


def dot(a, b):
    return lax.dot_general(a, b, (((1,), (0,)), ((), ())), preferred_element_type=F32)


def dot_nt(a, b):
    return lax.dot_general(a, b, (((1,), (1,)), ((), ())), preferred_element_type=F32)


def to_rows(column, eye):
    return jnp.sum(jnp.where(eye, column, 0.0), axis=0, keepdims=True)


def to_columns(row, eye):
    return jnp.sum(jnp.where(eye, row, 0.0), axis=1, keepdims=True)


def kernel(
    hid_hbm,
    mod_hbm,
    proj_hbm,
    bias_hbm,
    ker1_hbm,
    bias1_hbm,
    gain_hbm,
    ker2_hbm,
    bias2_hbm,
    counts_hbm,
    plan_hbm,
    out,
    hid,
    mod,
    proj,
    bias,
    counts,
    plan,
    ker1,
    bias1,
    gain,
    bias2,
    stats,
    stats_in,
    weight,
    gains,
    share,
    share_out,
    share_in,
    base,
    scale,
    tok,
    tok_out,
    tok_in,
    spread,
    onehot,
    sendbuf,
    recv,
    y,
    mover,
    mask,
    taps,
    w1,
    lhs,
    acc,
    feat,
    mix,
    local_sem,
    stat_send,
    stat_recv,
    share_send,
    share_recv,
    tok_send,
    tok_recv,
    out_send,
    out_recv,
    tap_sem,
):
    my_seq = lax.axis_index("seq")
    my_row = lax.axis_index("row")

    loads = [
        pltpu.make_async_copy(counts_hbm, counts, local_sem.at[0]),
        pltpu.make_async_copy(plan_hbm, plan, local_sem.at[1]),
        pltpu.make_async_copy(proj_hbm, proj, local_sem.at[2]),
        pltpu.make_async_copy(mod_hbm.at[:, 1, :], mod.at[1], local_sem.at[3]),
        pltpu.make_async_copy(mod_hbm.at[:, 0, :], mod.at[0], local_sem.at[13]),
        pltpu.make_async_copy(bias_hbm, bias, local_sem.at[4]),
        pltpu.make_async_copy(ker1_hbm, ker1, local_sem.at[5]),
        pltpu.make_async_copy(bias1_hbm, bias1, local_sem.at[6]),
        pltpu.make_async_copy(gain_hbm, gain, local_sem.at[7]),
        pltpu.make_async_copy(bias2_hbm, bias2, local_sem.at[8]),
    ]
    hid_loads = [
        pltpu.make_async_copy(
            hid_hbm.at[pl.ds(QF * q, QF)], hid.at[pl.ds(QF * q, QF)], local_sem.at[9 + q]
        )
        for q in range(ROW)
    ]
    for copy in [loads[3], loads[4], loads[2]] + hid_loads + loads[0:2] + [loads[5]]:
        copy.start()

    barrier = pltpu.get_barrier_semaphore()
    for i in range(1, ROW):
        pl.semaphore_signal(
            barrier,
            inc=1,
            device_id=(my_seq, lax.rem(my_row + i, ROW)),
            device_id_type=MESH,
        )

    def greet(i, carry):
        pl.semaphore_signal(
            barrier,
            inc=1,
            device_id=(lax.rem(my_seq + i, SEQ), my_row),
            device_id_type=MESH,
        )
        return carry

    lax.fori_loop(1, SEQ, greet, 0)

    eye = iota((QF, QF), 0) == iota((QF, QF), 1)

    for copy in loads[0:2]:
        copy.wait()
    counts_row = counts[...].astype(F32)
    square = (REQ, REQ)
    counts_col = jnp.sum(
        jnp.where(iota(square, 0) == iota(square, 1), counts_row, 0.0), axis=1, keepdims=True
    )
    ends_col = jnp.sum(
        jnp.where(iota(square, 1) <= iota(square, 0), counts_row, 0.0), axis=1, keepdims=True
    )
    starts_col = ends_col - counts_col
    wide = (REQ, 2 * REQ)
    request_lane = lax.rem(iota(wide, 1), REQ)
    ends_row = jnp.sum(
        jnp.where(iota(wide, 0) <= request_lane, counts_col, 0.0), axis=0, keepdims=True
    )
    starts_row = jnp.sum(
        jnp.where(iota(wide, 0) < request_lane, counts_col, 0.0), axis=0, keepdims=True
    )

    for copy in loads[2:6]:
        copy.wait()

    lanes = (Z * 4, 2 * Z * 4)
    lane = lax.rem(iota(lanes, 1), 4 * Z)
    wanted = lax.rem(lane // Z, 2) * (2 * Z) + (lane // (2 * Z)) * Z + lax.rem(lane, Z)
    reorder = jnp.where(iota(lanes, 0) == wanted, 1.0, 0.0).astype(BF16)
    weight[...] = lax.dot_general(
        proj[...], reorder, (((0,), (0,)), ((), ())), preferred_element_type=F32
    ).astype(BF16)
    bias_hi, bias_lo = split_bf16(jnp.broadcast_to(bias[...], (16, 4 * Z)))
    bias_lo2 = (
        jnp.broadcast_to(bias[...], (16, 4 * Z)) - bias_hi.astype(F32) - bias_lo.astype(F32)
    ).astype(BF16)
    bias_row = (dot(bias_hi, reorder) + dot(bias_lo, reorder) + dot(bias_lo2, reorder))[0:1, :]

    gains[0:REQ, :], gains[REQ : 2 * REQ, :] = split_bf16(1.0 + mod[1])
    gains[2 * REQ : 3 * REQ, :], gains[3 * REQ : 4 * REQ, :] = split_bf16(mod[0])
    by_part = dot(gains[...], weight[...])
    gain_weight = by_part[0:REQ] + by_part[REQ : 2 * REQ]
    shift_weight = by_part[2 * REQ : 3 * REQ] + by_part[3 * REQ : 4 * REQ]
    share[...] = jnp.where(iota((REQ, 128), 1) < 64, gain_weight, shift_weight)
    share_out[...] = share[...].astype(BF16)

    members = []
    for q in range(ROW):
        frame = (iota((QF, 2 * REQ), 0) + QF * q).astype(F32)
        members.append(
            jnp.where(
                jnp.logical_and(frame >= starts_row, frame < ends_row), 1.0, 0.0
            ).astype(BF16)
        )

    share_copies, stat_copies, tok_copies = [], [], []

    def to_row_peers(source, target, send_sem, recv_sem, copies):
        for i in range(1, ROW):
            copy = pltpu.make_async_remote_copy(
                src_ref=source,
                dst_ref=target(i - 1),
                send_sem=send_sem(i - 1),
                recv_sem=recv_sem(i - 1),
                device_id=(my_seq, lax.rem(my_row + i, ROW)),
                device_id_type=MESH,
            )
            copy.start()
            copies.append(copy)

    def send_quarter(q):
        to_row_peers(
            tok_out.at[q],
            lambda n: tok_in.at[n, q],
            lambda n: tok_send.at[q, n],
            lambda n: tok_recv.at[q, n],
            tok_copies,
        )

    half = iota((QF // 2, 128), 1) < 64
    share_rows = jnp.concatenate(split_bf16(gain_weight), axis=0)
    means = []
    for q in range(ROW):
        hid_loads[q].wait()
        h = hid[QF * q : QF * (q + 1), :].astype(F32)
        one = jnp.sum(h, axis=1, keepdims=True)
        two = jnp.sum(h * h, axis=1, keepdims=True)
        means.append(one / DL)
        stats[q : q + 1, :] = to_rows(one, eye)
        stats[ROW + q : ROW + q + 1, :] = to_rows(two, eye)

    def project(q):
        h = hid[QF * q : QF * (q + 1), :].astype(F32)
        x_hi, x_lo = split_bf16(h * dot(members[q], gains[0 : 2 * REQ, :]))
        both = dot(jnp.concatenate([x_hi, x_lo], axis=0), weight[...])
        projected = both[0:QF] + both[QF : 2 * QF] - means[q] * dot(members[q], share_rows)
        tok[q] = jnp.where(half, projected[0 : QF // 2], projected[QF // 2 : QF])
        tok_out[q] = tok[q].astype(BF16)

    project(0)
    project(1)
    pl.semaphore_wait(barrier, ROW - 1 + SEQ - 1)
    to_row_peers(
        share_out,
        lambda n: share_in.at[n],
        lambda n: share_send.at[n],
        lambda n: share_recv.at[n],
        share_copies,
    )
    to_row_peers(
        stats,
        lambda n: stats_in.at[n],
        lambda n: stat_send.at[n],
        lambda n: stat_recv.at[n],
        stat_copies,
    )
    send_quarter(0)
    send_quarter(1)
    project(2)
    send_quarter(2)
    project(3)
    send_quarter(3)

    for copy in loads[6:]:
        copy.start()
    for t in range(3):
        for p in range(2):
            for e in range(3):
                for i in range(2):
                    pltpu.make_async_copy(
                        ker2_hbm.at[9 * t + 3 * (p - i + 1) + e],
                        taps.at[t, pl.ds((3 * p + e) * C, C), pl.ds(i * C, C)],
                        tap_sem.at[t],
                    ).start()


    plan_row = plan[...]
    plan_f32 = plan_row.astype(F32)
    frame_row = iota((1, FRAMES), 1)
    frame_f32 = frame_row.astype(F32)
    rank = jnp.zeros((1, FRAMES), F32)
    for q in range(ROW):
        plan_col = to_columns(plan_f32[:, QF * q : QF * (q + 1)], eye)
        before = iota((QF, FRAMES), 0) + QF * q < iota((QF, FRAMES), 1)
        rank += jnp.sum(
            jnp.where(jnp.logical_and(plan_col == plan_f32, before), 1.0, 0.0),
            axis=0,
            keepdims=True,
        )
    code = jnp.where(
        plan_row - (plan_row // ROW) * ROW == my_row,
        (plan_row // ROW).astype(F32) * CAP + rank,
        -1.0,
    )
    by_request = (REQ, FRAMES)
    frame_of = iota(by_request, 1).astype(F32)
    first = jnp.sum(
        jnp.where(
            jnp.logical_and(frame_of >= starts_col, frame_of < ends_col), starts_col, 0.0
        ),
        axis=0,
        keepdims=True,
    )
    shifted = []
    for back in range(5):
        if back == 0:
            shifted.append(code)
            continue
        code_ahead = pltpu.roll(jnp.broadcast_to(code, (8, FRAMES)), FRAMES - back, 1)[0:1]
        first_ahead = pltpu.roll(jnp.broadcast_to(first, (8, FRAMES)), FRAMES - back, 1)[0:1]
        shifted.append(
            jnp.where(
                jnp.logical_and(first_ahead <= frame_f32, frame_row < FRAMES - back),
                code_ahead,
                -1.0,
            )
        )

    def wanted_by(rows, halves):
        latent_row = halves - (halves // 5) * 5
        picked = jnp.broadcast_to(shifted[0], (rows, FRAMES))
        for back in range(1, 5):
            picked = jnp.where(latent_row == 4 - back, shifted[back], picked)
        return picked - (halves // 5).astype(F32)

    own = wanted_by(24, iota((24, FRAMES), 0))
    mask[...] = jnp.broadcast_to(
        jnp.sum(jnp.where(own == (my_seq * CAP).astype(F32), 1.0, 0.0), axis=1, keepdims=True),
        (24, 128),
    )
    rows = iota((80, FRAMES), 0)
    table = jnp.concatenate(
        [
            wanted_by(80, 2 * lax.rem(rows, 10) + high) - (rows // 10 * CAP).astype(F32)
            for high in range(2)
        ],
        axis=1,
    )
    for n in range(SEQ // 8):
        onehot[80 * n : 80 * (n + 1), :] = jnp.where(table == float(8 * CAP * n), 1.0, 0.0).astype(
            BF16
        )

    for copy in share_copies + stat_copies:
        copy.wait_recv()
    total = stats[...] + stats_in[0] + stats_in[1] + stats_in[2]
    average_row = total[0:ROW] / D
    inverse_row = lax.rsqrt(total[ROW : 2 * ROW] / D - average_row * average_row + EPSILON)
    shares = [share[...]] + [share_in[n].astype(F32) for n in range(ROW - 1)]
    left_half = iota((REQ, 128), 1) < 64
    shift_total = shares[0] + shares[1] + shares[2] + shares[3]
    spreads = [jnp.where(left_half, v, pltpu.roll(v, 64, 1)) for v in shares]
    spreads.append(jnp.where(left_half, pltpu.roll(shift_total, 64, 1), shift_total))
    spreads = jnp.concatenate(split_bf16(jnp.concatenate(spreads, axis=1)), axis=0)
    sums = [stats, stats_in.at[0], stats_in.at[1], stats_in.at[2]]
    for q in range(ROW):
        by_frame = dot(members[q], spreads)
        inverse = to_columns(inverse_row[q : q + 1], eye)
        rest = by_frame[:, 512:640] + bias_row
        for n in range(ROW):
            offset = (sums[n][q : q + 1, :] / DL - average_row[q : q + 1]) * inverse_row[q : q + 1]
            rest += to_columns(offset, eye) * by_frame[:, 128 * n : 128 * (n + 1)]
        base[q] = jnp.where(half, rest[0 : QF // 2], rest[QF // 2 : QF])
        scale[q] = jnp.where(half, inverse[0 : QF // 2], inverse[QF // 2 : QF])

    for copy in loads[6:]:
        copy.wait()

    def fill(start, a, columns):
        for n, (position, q) in enumerate(columns):
            for i in range(2):
                for r in range(2):
                    e = position - r + 1
                    if 0 <= e <= 2:
                        block = ker1[9 * a + 3 * (q - i + 1) + e]
                    else:
                        block = jnp.zeros((Z, C), BF16)
                    w1[start + Z * n : start + Z * (n + 1), (2 * i + r) * C : (2 * i + r + 1) * C] = (
                        block
                    )

    own = [(0, 0), (0, 1), (1, 0), (1, 1)]
    rim = [(2, 0), (2, 1), (-1, 0), (-1, 1)]
    for start, a, columns in (
        (0, 0, own),
        (64, 1, own),
        (128, 0, rim),
        (192, 2, own),
        (256, 1, rim),
        (320, 2, rim),
    ):
        fill(start, a, columns)

    moved = (256, 640)
    to_row, from_row = iota(moved, 0), iota(moved, 1)
    group, place = to_row // 16, lax.rem(to_row, 16) * 10
    low = lax.rem(group, 4) * 5 + group // 4
    high = low + 1
    mover[...] = jnp.where(
        jnp.logical_or(
            from_row == lax.rem(low, 2) * 160 + place + low // 2,
            from_row == (2 + lax.rem(high, 2)) * 160 + place + high // 2,
        ),
        1.0,
        0.0,
    ).astype(BF16)

    bias1_row = bias1[...].reshape(1, C)
    gain_row = gain[...].reshape(1, C)

    for q in range(ROW):
        for copy in tok_copies[(ROW - 1) * q : (ROW - 1) * (q + 1)]:
            copy.wait_recv()
        here = (
            (
                (
                    tok[q]
                    + tok_in[0, q].astype(F32)
                    + tok_in[1, q].astype(F32)
                    + tok_in[2, q].astype(F32)
                )
                * scale[q]
                + base[q]
            )
            .astype(BF16)
            .astype(F32)
        )
        there = pltpu.roll(here, 64, 1)
        low, high = jnp.where(half, here, 0.0), jnp.where(half, 0.0, here)
        low_moved, high_moved = jnp.where(half, there, 0.0), jnp.where(half, 0.0, there)
        for at, block in (
            (QF * q, low),
            (QF * q + 64, low_moved),
            (FRAMES + QF * q, high_moved),
            (FRAMES + QF * q + 64, high),
        ):
            spread[at : at + 64, :] = block.astype(BF16)
    for block in range(4):
        rows = slice(160 * block, 160 * (block + 1))
        sendbuf[16 * block : 16 * (block + 1)] = (
            dot(onehot[rows, :], spread[...]).astype(BF16).reshape(16, 5, 2, 128)
        )

    my_y, my_z, my_core = my_seq // 16, lax.rem(my_seq, 16) // 2, lax.rem(my_seq, 2)

    def swing(j, half_way):
        step = (j + 1) // 2
        return half_way + step * (2 * lax.rem(j, 2) - 1)

    def post(i, carry):
        to_z = lax.rem(my_z + swing(i // 8, 4), 8)
        to_y = lax.rem(my_y + swing(lax.rem(i, 8) // 2, 2), 4)
        to_core = lax.rem(my_core + 1 - lax.rem(i, 2), 2)
        to = to_y * 16 + to_z * 2 + to_core
        pltpu.make_async_remote_copy(
            src_ref=sendbuf.at[to],
            dst_ref=recv.at[my_seq],
            send_sem=out_send,
            recv_sem=out_recv,
            device_id=(to, my_row),
            device_id_type=MESH,
        ).start()
        return carry

    lax.fori_loop(0, SEQ - 1, post, 0)
    recv[my_seq] = sendbuf[my_seq]

    for t in range(3):
        pltpu.make_async_copy(taps.at[t], taps.at[t], tap_sem.at[t]).wait()
    arrived = recv.at[pl.ds(0, SEQ - 1)]
    pltpu.make_async_copy(arrived, arrived, out_recv).wait()
    left = iota((160, 128), 1) < 64
    for block in range(4):
        got = recv[16 * block : 16 * (block + 1)].reshape(160, 128).astype(F32)
        turned = pltpu.roll(got, 64, 1)
        parts = jnp.concatenate(
            [
                jnp.where(left, got, 0.0),
                jnp.where(left, turned, 0.0),
                jnp.where(left, 0.0, turned),
                jnp.where(left, 0.0, got),
            ],
            axis=0,
        ).astype(BF16)
        y[:, 16 * block : 16 * (block + 1), :] = (
            dot(mover[...], parts).astype(BF16).reshape(16, 16, 128)
        )

    rows = CAP * SEQ
    column = lax.rem(iota((rows, 128), 0), SEQ)
    lane = iota((rows, 128), 1)

    def rims(v):
        right = jnp.where(column == SEQ - 1, 0.0, pltpu.roll(v, rows - 1, 0))
        left = jnp.where(column == 0, 0.0, pltpu.roll(v, 1, 0))
        return jnp.where(lax.rem(lane, 64) < 32, right, left)

    wide = [y[CAP * t : CAP * (t + 1)].reshape(rows, 128).astype(F32) for t in range(4)]
    around = [rims(v) for v in wide]
    first_col = iota((SEQ, C), 0) == 0
    last_col = iota((SEQ, C), 0) == SEQ - 1
    xs = []
    for t in range(3):
        xs.append(
            jnp.concatenate(
                [wide[t], jnp.where(lane < 64, around[t], wide[t + 1]), around[t + 1]], axis=1
            ).astype(BF16)
        )

    def features(t):
        for p in range(2):
            cols = slice(2 * p * C, 2 * (p + 1) * C)
            feat[t, :, cols] = dot(xs[t], w1[:, cols])

    def activate(t):
        for k in range(CAP):
            live = 0.5 * mask[5 * k + t + 2 : 5 * k + t + 3, 0:1]
            here = slice(k * SEQ, (k + 1) * SEQ)
            for p in range(2):
                for r in range(2):
                    v = feat[t, here, (2 * p + r) * C : (2 * p + r + 1) * C] + bias1_row
                    factor = lax.rsqrt(jnp.mean(v * v, axis=1, keepdims=True) + EPSILON) * live
                    n = v * factor * gain_row
                    a = n + n * jnp.tanh(n)

                    def put(side, e, value):
                        lhs[
                            t,
                            side * rows + k * SEQ : side * rows + (k + 1) * SEQ,
                            (3 * p + e) * C : (3 * p + e + 1) * C,
                        ] = value.astype(BF16)

                    if r == 0:
                        put(0, 1, a)
                        put(1, 0, a)
                        put(1, 2, jnp.where(last_col, 0.0, pltpu.roll(a, SEQ - 1, 0)))
                    else:
                        put(0, 2, a)
                        put(1, 1, a)
                        put(0, 0, jnp.where(first_col, 0.0, pltpu.roll(a, 1, 0)))

    features(0)
    activate(0)
    for t in range(2):
        features(t + 1)
        product = dot(lhs[t], taps[t])
        if t == 0:
            acc[...] = product
        else:
            acc[...] += product
        activate(t + 1)

    both_bias = bias2[...].reshape(1, C) + bias1_row
    for n in range(3):
        product = dot(lhs[2], taps[2, :, 256 * n : 256 * (n + 1)])
        for part in range(2):
            at = 2 * n + part
            i, at_c = at // 3, 128 * (at % 3)
            for k in range(CAP):
                live = mask[5 * k + 4 : 5 * k + 5, 0:1]
                for r in range(2):
                    here = slice(r * rows + k * SEQ, r * rows + (k + 1) * SEQ)
                    col = (2 * i + r) * C + at_c
                    mix[part, k, pl.ds(r, SEQ, stride=2), :] = (
                        product[here, 128 * part : 128 * (part + 1)]
                        + acc[here, 128 * at : 128 * (at + 1)]
                        + feat[2, k * SEQ : (k + 1) * SEQ, col : col + 128]
                        + both_bias[:, at_c : at_c + 128]
                    ) * live
                out[k, i, :, at_c : at_c + 128] = mix[part, k].astype(BF16)

    for copy in share_copies + stat_copies + tok_copies:
        copy.wait_send()
    sent = sendbuf.at[pl.ds(0, SEQ - 1)]
    pltpu.make_async_copy(sent, sent, out_send).wait()


def shards(
    hidden,
    modulation,
    projection,
    projection_bias,
    input_kernel,
    input_bias,
    norm_gain,
    block_kernel,
    block_bias,
    frame_counts,
    decoder_plan,
):
    hbm = pl.BlockSpec(memory_space=pltpu.HBM)
    return pl.pallas_call(
        kernel,
        out_shape=jax.ShapeDtypeStruct((CAP, 2, 2 * SEQ, C), BF16),
        in_specs=[hbm] * 11,
        out_specs=pl.BlockSpec(memory_space=pltpu.VMEM),
        scratch_shapes=[
            pltpu.VMEM((FRAMES, DL), BF16),
            pltpu.VMEM((2, REQ, DL), F32),
            pltpu.VMEM((4 * Z, DL), BF16),
            pltpu.VMEM((1, 4 * Z), F32),
            pltpu.VMEM((1, REQ), jnp.int32),
            pltpu.VMEM((1, FRAMES), jnp.int32),
            pltpu.VMEM((27, Z, C), BF16),
            pltpu.VMEM((C,), F32),
            pltpu.VMEM((C,), F32),
            pltpu.VMEM((C,), F32),
            pltpu.VMEM((2 * ROW, QF), F32),
            pltpu.VMEM((ROW - 1, 2 * ROW, QF), F32),
            pltpu.VMEM((DL, 128), BF16),
            pltpu.VMEM((4 * REQ, DL), BF16),
            pltpu.VMEM((REQ, 128), F32),
            pltpu.VMEM((REQ, 128), BF16),
            pltpu.VMEM((ROW - 1, REQ, 128), BF16),
            pltpu.VMEM((ROW, QF // 2, 128), F32),
            pltpu.VMEM((ROW, QF // 2, 128), F32),
            pltpu.VMEM((ROW, QF // 2, 128), F32),
            pltpu.VMEM((ROW, QF // 2, 128), BF16),
            pltpu.VMEM((ROW - 1, ROW, QF // 2, 128), BF16),
            pltpu.VMEM((2 * FRAMES, 128), BF16),
            pltpu.VMEM((10 * SEQ, 2 * FRAMES), BF16),
            pltpu.VMEM((SEQ, 5, 2, 128), BF16),
            pltpu.VMEM((SEQ, 5, 2, 128), BF16),
            pltpu.VMEM((16, SEQ, 128), BF16),
            pltpu.VMEM((256, 640), BF16),
            pltpu.VMEM((24, 128), F32),
            pltpu.VMEM((3, 6 * C, 2 * C), BF16),
            pltpu.VMEM((24 * Z, 4 * C), BF16),
            pltpu.VMEM((3, 2 * CAP * SEQ, 6 * C), BF16),
            pltpu.VMEM((2 * CAP * SEQ, 2 * C), F32),
            pltpu.VMEM((3, CAP * SEQ, 4 * C), F32),
            pltpu.VMEM((2, CAP, 2 * SEQ, 128), F32),
            pltpu.SemaphoreType.DMA((10 + ROW,)),
            pltpu.SemaphoreType.DMA((ROW - 1,)),
            pltpu.SemaphoreType.DMA((ROW - 1,)),
            pltpu.SemaphoreType.DMA((ROW - 1,)),
            pltpu.SemaphoreType.DMA((ROW - 1,)),
            pltpu.SemaphoreType.DMA((ROW, ROW - 1)),
            pltpu.SemaphoreType.DMA((ROW, ROW - 1)),
            pltpu.SemaphoreType.DMA,
            pltpu.SemaphoreType.DMA,
            pltpu.SemaphoreType.DMA((3,)),
        ],
        compiler_params=pltpu.CompilerParams(
            collective_id=0, has_side_effects=True, vmem_limit_bytes=44 << 20
        ),
    )(*[pltpu.with_memory_space_constraint(x, pltpu.HBM) for x in (
        hidden.reshape(FRAMES, DL),
        modulation,
        projection.T,
        projection_bias.reshape(1, 4 * Z),
        input_kernel,
        input_bias,
        norm_gain,
        block_kernel,
        block_bias,
        frame_counts.reshape(1, REQ),
        decoder_plan.reshape(1, FRAMES),
    )])


def solution(mesh):
    placed = (
        P(None, "seq", "row"),
        P(None, None, "row"),
        P("row", None),
        P(),
        P(),
        P(),
        P(),
        P(),
        P(),
        P(),
        P(),
    )
    return jax.shard_map(
        shards,
        mesh=mesh,
        in_specs=placed,
        out_specs=P(("seq", "row"), None, None, None),
        check_vma=False,
    )
```

```python
import functools

import jax
import jax.numpy as jnp
from jax import lax
from jax.experimental import pallas as pl
from jax.experimental.pallas import tpu as pltpu
from jax.sharding import PartitionSpec as P

MESH = pl.DeviceIdType.MESH
F32 = jnp.float32
BF16 = jnp.bfloat16

D = 5120
DL = 1280
Z = 16
C = 384
CAP = 4
FRAMES = 512
REQ = 64
SEQ = 64
ROW = 4
QF = FRAMES // ROW
EPSILON = 1e-06


def iota(shape, dim):
    return lax.broadcasted_iota(jnp.int32, shape, dim)


def split_bf16(x):
    high = x.astype(BF16)
    return high, (x - high.astype(F32)).astype(BF16)


def dot(a, b):
    return lax.dot_general(a, b, (((1,), (0,)), ((), ())), preferred_element_type=F32)


def dot_nt(a, b):
    return lax.dot_general(a, b, (((1,), (1,)), ((), ())), preferred_element_type=F32)


def to_rows(column, eye):
    return jnp.sum(jnp.where(eye, column, 0.0), axis=0, keepdims=True)


def to_columns(row, eye):
    return jnp.sum(jnp.where(eye, row, 0.0), axis=1, keepdims=True)


def kernel(
    hid_hbm,
    mod_hbm,
    proj_hbm,
    bias_hbm,
    ker1_hbm,
    bias1_hbm,
    gain_hbm,
    ker2_hbm,
    bias2_hbm,
    counts_hbm,
    plan_hbm,
    out,
    hid,
    mod,
    proj,
    bias,
    counts,
    plan,
    ker1,
    bias1,
    gain,
    bias2,
    stats,
    stats_in,
    weight,
    gains,
    share,
    share_out,
    share_in,
    base,
    scale,
    tok,
    tok_out,
    tok_in,
    spread,
    onehot,
    sendbuf,
    recv,
    y,
    mover,
    mask,
    taps,
    w1,
    lhs,
    acc,
    feat,
    mix,
    local_sem,
    stat_send,
    stat_recv,
    share_send,
    share_recv,
    tok_send,
    tok_recv,
    out_send,
    out_recv,
    tap_sem,
):
    my_seq = lax.axis_index("seq")
    my_row = lax.axis_index("row")

    loads = [
        pltpu.make_async_copy(counts_hbm, counts, local_sem.at[0]),
        pltpu.make_async_copy(plan_hbm, plan, local_sem.at[1]),
        pltpu.make_async_copy(proj_hbm, proj, local_sem.at[2]),
        pltpu.make_async_copy(mod_hbm.at[:, 1, :], mod.at[1], local_sem.at[3]),
        pltpu.make_async_copy(mod_hbm.at[:, 0, :], mod.at[0], local_sem.at[13]),
        pltpu.make_async_copy(bias_hbm, bias, local_sem.at[4]),
        pltpu.make_async_copy(ker1_hbm, ker1, local_sem.at[5]),
        pltpu.make_async_copy(bias1_hbm, bias1, local_sem.at[6]),
        pltpu.make_async_copy(gain_hbm, gain, local_sem.at[7]),
        pltpu.make_async_copy(bias2_hbm, bias2, local_sem.at[8]),
    ]
    hid_loads = [
        pltpu.make_async_copy(
            hid_hbm.at[pl.ds(QF * q, QF)], hid.at[pl.ds(QF * q, QF)], local_sem.at[9 + q]
        )
        for q in range(ROW)
    ]
    for copy in [loads[3], loads[4], loads[2]] + hid_loads + loads[0:2] + [loads[5]]:
        copy.start()

    barrier = pltpu.get_barrier_semaphore()
    for i in range(1, ROW):
        pl.semaphore_signal(
            barrier,
            inc=1,
            device_id=(my_seq, lax.rem(my_row + i, ROW)),
            device_id_type=MESH,
        )

    my_y, my_z, my_core = my_seq // 16, lax.rem(my_seq, 16) // 2, lax.rem(my_seq, 2)
    lines = [
        lax.rem(my_y + y, 4) * 16 + lax.rem(my_core + core, 2) for y in (2, 3, 1, 0) for core in (1, 0)
    ]

    def every_other(act):
        def along(j, carry):
            step = (j + 1) // 2
            to_z = lax.rem(my_z + 4 + step * (2 * lax.rem(j, 2) - 1), 8) * 2
            for line in lines:
                act(line + to_z)
            return carry

        lax.fori_loop(0, 7, along, 0)
        for line in lines[:-1]:
            act(line + my_z * 2)

    def greet(to):
        pl.semaphore_signal(barrier, inc=1, device_id=(to, my_row), device_id_type=MESH)

    every_other(greet)

    eye = iota((QF, QF), 0) == iota((QF, QF), 1)

    for copy in loads[0:2]:
        copy.wait()
    counts_row = counts[...].astype(F32)
    square = (REQ, REQ)
    counts_col = jnp.sum(
        jnp.where(iota(square, 0) == iota(square, 1), counts_row, 0.0), axis=1, keepdims=True
    )
    ends_col = jnp.sum(
        jnp.where(iota(square, 1) <= iota(square, 0), counts_row, 0.0), axis=1, keepdims=True
    )
    starts_col = ends_col - counts_col
    wide = (REQ, 2 * REQ)
    request_lane = lax.rem(iota(wide, 1), REQ)
    ends_row = jnp.sum(
        jnp.where(iota(wide, 0) <= request_lane, counts_col, 0.0), axis=0, keepdims=True
    )
    starts_row = jnp.sum(
        jnp.where(iota(wide, 0) < request_lane, counts_col, 0.0), axis=0, keepdims=True
    )

    for copy in loads[2:6]:
        copy.wait()

    lanes = (Z * 4, 2 * Z * 4)
    lane = lax.rem(iota(lanes, 1), 4 * Z)
    wanted = lax.rem(lane // Z, 2) * (2 * Z) + (lane // (2 * Z)) * Z + lax.rem(lane, Z)
    reorder = jnp.where(iota(lanes, 0) == wanted, 1.0, 0.0).astype(BF16)
    weight[...] = lax.dot_general(
        proj[...], reorder, (((0,), (0,)), ((), ())), preferred_element_type=F32
    ).astype(BF16)
    bias_hi, bias_lo = split_bf16(jnp.broadcast_to(bias[...], (16, 4 * Z)))
    bias_lo2 = (
        jnp.broadcast_to(bias[...], (16, 4 * Z)) - bias_hi.astype(F32) - bias_lo.astype(F32)
    ).astype(BF16)
    bias_row = (dot(bias_hi, reorder) + dot(bias_lo, reorder) + dot(bias_lo2, reorder))[0:1, :]

    gains[0:REQ, :], gains[REQ : 2 * REQ, :] = split_bf16(1.0 + mod[1])
    gains[2 * REQ : 3 * REQ, :], gains[3 * REQ : 4 * REQ, :] = split_bf16(mod[0])
    by_part = dot(gains[...], weight[...])
    gain_weight = by_part[0:REQ] + by_part[REQ : 2 * REQ]
    shift_weight = by_part[2 * REQ : 3 * REQ] + by_part[3 * REQ : 4 * REQ]
    share[...] = jnp.where(iota((REQ, 128), 1) < 64, gain_weight, shift_weight)
    share_out[...] = share[...].astype(BF16)

    members = []
    for q in range(ROW):
        frame = (iota((QF, 2 * REQ), 0) + QF * q).astype(F32)
        members.append(
            jnp.where(
                jnp.logical_and(frame >= starts_row, frame < ends_row), 1.0, 0.0
            ).astype(BF16)
        )

    share_copies, stat_copies, tok_copies = [], [], []

    def to_row_peers(source, target, send_sem, recv_sem, copies):
        for i in range(1, ROW):
            copy = pltpu.make_async_remote_copy(
                src_ref=source,
                dst_ref=target(i - 1),
                send_sem=send_sem(i - 1),
                recv_sem=recv_sem(i - 1),
                device_id=(my_seq, lax.rem(my_row + i, ROW)),
                device_id_type=MESH,
            )
            copy.start()
            copies.append(copy)

    def send_quarter(q):
        to_row_peers(
            tok_out.at[q],
            lambda n: tok_in.at[n, q],
            lambda n: tok_send.at[q, n],
            lambda n: tok_recv.at[q, n],
            tok_copies,
        )

    half = iota((QF // 2, 128), 1) < 64
    share_rows = jnp.concatenate(split_bf16(gain_weight), axis=0)
    means = []
    for q in range(ROW):
        hid_loads[q].wait()
        h = hid[QF * q : QF * (q + 1), :].astype(F32)
        one = jnp.sum(h, axis=1, keepdims=True)
        two = jnp.sum(h * h, axis=1, keepdims=True)
        means.append(one / DL)
        stats[q : q + 1, :] = to_rows(one, eye)
        stats[ROW + q : ROW + q + 1, :] = to_rows(two, eye)

    def project(q):
        h = hid[QF * q : QF * (q + 1), :].astype(F32)
        x_hi, x_lo = split_bf16(h * dot(members[q], gains[0 : 2 * REQ, :]))
        both = dot(jnp.concatenate([x_hi, x_lo], axis=0), weight[...])
        projected = both[0:QF] + both[QF : 2 * QF] - means[q] * dot(members[q], share_rows)
        tok[q] = jnp.where(half, projected[0 : QF // 2], projected[QF // 2 : QF])
        tok_out[q] = tok[q].astype(BF16)

    pl.semaphore_wait(barrier, ROW - 1 + SEQ - 1)
    to_row_peers(
        share_out,
        lambda n: share_in.at[n],
        lambda n: share_send.at[n],
        lambda n: share_recv.at[n],
        share_copies,
    )
    to_row_peers(
        stats,
        lambda n: stats_in.at[n],
        lambda n: stat_send.at[n],
        lambda n: stat_recv.at[n],
        stat_copies,
    )
    project(0)
    send_quarter(0)
    project(1)
    send_quarter(1)
    project(2)
    send_quarter(2)
    project(3)
    send_quarter(3)

    for copy in loads[6:]:
        copy.start()
    for t in range(3):
        for p in range(2):
            for e in range(3):
                for i in range(2):
                    pltpu.make_async_copy(
                        ker2_hbm.at[9 * t + 3 * (p - i + 1) + e],
                        taps.at[t, pl.ds((3 * p + e) * C, C), pl.ds(i * C, C)],
                        tap_sem.at[t],
                    ).start()


    plan_row = plan[...]
    plan_f32 = plan_row.astype(F32)
    frame_row = iota((1, FRAMES), 1)
    frame_f32 = frame_row.astype(F32)
    rank = jnp.zeros((1, FRAMES), F32)
    for q in range(ROW):
        plan_col = to_columns(plan_f32[:, QF * q : QF * (q + 1)], eye)
        before = iota((QF, FRAMES), 0) + QF * q < iota((QF, FRAMES), 1)
        rank += jnp.sum(
            jnp.where(jnp.logical_and(plan_col == plan_f32, before), 1.0, 0.0),
            axis=0,
            keepdims=True,
        )
    code = jnp.where(
        plan_row - (plan_row // ROW) * ROW == my_row,
        (plan_row // ROW).astype(F32) * CAP + rank,
        -1.0,
    )
    by_request = (REQ, FRAMES)
    frame_of = iota(by_request, 1).astype(F32)
    first = jnp.sum(
        jnp.where(
            jnp.logical_and(frame_of >= starts_col, frame_of < ends_col), starts_col, 0.0
        ),
        axis=0,
        keepdims=True,
    )
    shifted = []
    for back in range(5):
        if back == 0:
            shifted.append(code)
            continue
        code_ahead = pltpu.roll(jnp.broadcast_to(code, (8, FRAMES)), FRAMES - back, 1)[0:1]
        first_ahead = pltpu.roll(jnp.broadcast_to(first, (8, FRAMES)), FRAMES - back, 1)[0:1]
        shifted.append(
            jnp.where(
                jnp.logical_and(first_ahead <= frame_f32, frame_row < FRAMES - back),
                code_ahead,
                -1.0,
            )
        )

    def wanted_by(rows, halves):
        latent_row = halves - (halves // 5) * 5
        picked = jnp.broadcast_to(shifted[0], (rows, FRAMES))
        for back in range(1, 5):
            picked = jnp.where(latent_row == 4 - back, shifted[back], picked)
        return picked - (halves // 5).astype(F32)

    own = wanted_by(24, iota((24, FRAMES), 0))
    mask[...] = jnp.broadcast_to(
        jnp.sum(jnp.where(own == (my_seq * CAP).astype(F32), 1.0, 0.0), axis=1, keepdims=True),
        (24, 128),
    )
    rows = iota((80, FRAMES), 0)
    table = jnp.concatenate(
        [
            wanted_by(80, 2 * lax.rem(rows, 10) + high) - (rows // 10 * CAP).astype(F32)
            for high in range(2)
        ],
        axis=1,
    )
    for n in range(SEQ // 8):
        onehot[80 * n : 80 * (n + 1), :] = jnp.where(table == float(8 * CAP * n), 1.0, 0.0).astype(
            BF16
        )

    for copy in share_copies + stat_copies:
        copy.wait_recv()
    total = stats[...] + stats_in[0] + stats_in[1] + stats_in[2]
    average_row = total[0:ROW] / D
    inverse_row = lax.rsqrt(total[ROW : 2 * ROW] / D - average_row * average_row + EPSILON)
    shares = [share[...]] + [share_in[n].astype(F32) for n in range(ROW - 1)]
    left_half = iota((REQ, 128), 1) < 64
    shift_total = shares[0] + shares[1] + shares[2] + shares[3]
    spreads = [jnp.where(left_half, v, pltpu.roll(v, 64, 1)) for v in shares]
    spreads.append(jnp.where(left_half, pltpu.roll(shift_total, 64, 1), shift_total))
    spreads = jnp.concatenate(split_bf16(jnp.concatenate(spreads, axis=1)), axis=0)
    sums = [stats, stats_in.at[0], stats_in.at[1], stats_in.at[2]]
    for q in range(ROW):
        by_frame = dot(members[q], spreads)
        inverse = to_columns(inverse_row[q : q + 1], eye)
        rest = by_frame[:, 512:640] + bias_row
        for n in range(ROW):
            offset = (sums[n][q : q + 1, :] / DL - average_row[q : q + 1]) * inverse_row[q : q + 1]
            rest += to_columns(offset, eye) * by_frame[:, 128 * n : 128 * (n + 1)]
        base[q] = jnp.where(half, rest[0 : QF // 2], rest[QF // 2 : QF])
        scale[q] = jnp.where(half, inverse[0 : QF // 2], inverse[QF // 2 : QF])

    for copy in loads[6:]:
        copy.wait()

    def fill(start, a, columns):
        for n, (position, q) in enumerate(columns):
            for i in range(2):
                for r in range(2):
                    e = position - r + 1
                    if 0 <= e <= 2:
                        block = ker1[9 * a + 3 * (q - i + 1) + e]
                    else:
                        block = jnp.zeros((Z, C), BF16)
                    w1[start + Z * n : start + Z * (n + 1), (2 * i + r) * C : (2 * i + r + 1) * C] = (
                        block
                    )

    own = [(0, 0), (0, 1), (1, 0), (1, 1)]
    rim = [(2, 0), (2, 1), (-1, 0), (-1, 1)]
    for start, a, columns in (
        (0, 0, own),
        (64, 1, own),
        (128, 0, rim),
        (192, 2, own),
        (256, 1, rim),
        (320, 2, rim),
    ):
        fill(start, a, columns)

    moved = (256, 640)
    to_row, from_row = iota(moved, 0), iota(moved, 1)
    group, place = to_row // 16, lax.rem(to_row, 16) * 10
    low = lax.rem(group, 4) * 5 + group // 4
    high = low + 1
    mover[...] = jnp.where(
        jnp.logical_or(
            from_row == lax.rem(low, 2) * 160 + place + low // 2,
            from_row == (2 + lax.rem(high, 2)) * 160 + place + high // 2,
        ),
        1.0,
        0.0,
    ).astype(BF16)

    bias1_row = bias1[...].reshape(1, C)
    gain_row = gain[...].reshape(1, C)

    for q in range(ROW):
        for copy in tok_copies[(ROW - 1) * q : (ROW - 1) * (q + 1)]:
            copy.wait_recv()
        here = (
            (
                (
                    tok[q]
                    + tok_in[0, q].astype(F32)
                    + tok_in[1, q].astype(F32)
                    + tok_in[2, q].astype(F32)
                )
                * scale[q]
                + base[q]
            )
            .astype(BF16)
            .astype(F32)
        )
        there = pltpu.roll(here, 64, 1)
        low, high = jnp.where(half, here, 0.0), jnp.where(half, 0.0, here)
        low_moved, high_moved = jnp.where(half, there, 0.0), jnp.where(half, 0.0, there)
        for at, block in (
            (QF * q, low),
            (QF * q + 64, low_moved),
            (FRAMES + QF * q, high_moved),
            (FRAMES + QF * q + 64, high),
        ):
            spread[at : at + 64, :] = block.astype(BF16)
    for block in range(4):
        rows = slice(160 * block, 160 * (block + 1))
        sendbuf[16 * block : 16 * (block + 1)] = (
            dot(onehot[rows, :], spread[...]).astype(BF16).reshape(16, 5, 2, 128)
        )

    def post(to):
        pltpu.make_async_remote_copy(
            src_ref=sendbuf.at[to],
            dst_ref=recv.at[my_seq],
            send_sem=out_send,
            recv_sem=out_recv,
            device_id=(to, my_row),
            device_id_type=MESH,
        ).start()

    every_other(post)
    recv[my_seq] = sendbuf[my_seq]

    for t in range(3):
        pltpu.make_async_copy(taps.at[t], taps.at[t], tap_sem.at[t]).wait()
    arrived = recv.at[pl.ds(0, SEQ - 1)]
    pltpu.make_async_copy(arrived, arrived, out_recv).wait()
    left = iota((160, 128), 1) < 64
    for block in range(4):
        got = recv[16 * block : 16 * (block + 1)].reshape(160, 128).astype(F32)
        turned = pltpu.roll(got, 64, 1)
        parts = jnp.concatenate(
            [
                jnp.where(left, got, 0.0),
                jnp.where(left, turned, 0.0),
                jnp.where(left, 0.0, turned),
                jnp.where(left, 0.0, got),
            ],
            axis=0,
        ).astype(BF16)
        y[:, 16 * block : 16 * (block + 1), :] = (
            dot(mover[...], parts).astype(BF16).reshape(16, 16, 128)
        )

    rows = CAP * SEQ
    column = lax.rem(iota((rows, 128), 0), SEQ)
    lane = iota((rows, 128), 1)

    def rims(v):
        right = jnp.where(column == SEQ - 1, 0.0, pltpu.roll(v, rows - 1, 0))
        left = jnp.where(column == 0, 0.0, pltpu.roll(v, 1, 0))
        return jnp.where(lax.rem(lane, 64) < 32, right, left)

    wide = [y[CAP * t : CAP * (t + 1)].reshape(rows, 128).astype(F32) for t in range(4)]
    around = [rims(v) for v in wide]
    first_col = iota((SEQ, C), 0) == 0
    last_col = iota((SEQ, C), 0) == SEQ - 1
    xs = []
    for t in range(3):
        xs.append(
            jnp.concatenate(
                [wide[t], jnp.where(lane < 64, around[t], wide[t + 1]), around[t + 1]], axis=1
            ).astype(BF16)
        )

    def features(t):
        for p in range(2):
            cols = slice(2 * p * C, 2 * (p + 1) * C)
            feat[t, :, cols] = dot(xs[t], w1[:, cols])

    def activate(t):
        for k in range(CAP):
            live = 0.5 * mask[5 * k + t + 2 : 5 * k + t + 3, 0:1]
            here = slice(k * SEQ, (k + 1) * SEQ)
            for p in range(2):
                for r in range(2):
                    v = feat[t, here, (2 * p + r) * C : (2 * p + r + 1) * C] + bias1_row
                    factor = lax.rsqrt(jnp.mean(v * v, axis=1, keepdims=True) + EPSILON) * live
                    n = v * factor * gain_row
                    a = n + n * jnp.tanh(n)

                    def put(side, e, value):
                        lhs[
                            t,
                            side * rows + k * SEQ : side * rows + (k + 1) * SEQ,
                            (3 * p + e) * C : (3 * p + e + 1) * C,
                        ] = value.astype(BF16)

                    if r == 0:
                        put(0, 1, a)
                        put(1, 0, a)
                        put(1, 2, jnp.where(last_col, 0.0, pltpu.roll(a, SEQ - 1, 0)))
                    else:
                        put(0, 2, a)
                        put(1, 1, a)
                        put(0, 0, jnp.where(first_col, 0.0, pltpu.roll(a, 1, 0)))

    features(0)
    activate(0)
    for t in range(2):
        features(t + 1)
        product = dot(lhs[t], taps[t])
        if t == 0:
            acc[...] = product
        else:
            acc[...] += product
        activate(t + 1)

    both_bias = bias2[...].reshape(1, C) + bias1_row
    for n in range(3):
        product = dot(lhs[2], taps[2, :, 256 * n : 256 * (n + 1)])
        for part in range(2):
            at = 2 * n + part
            i, at_c = at // 3, 128 * (at % 3)
            for k in range(CAP):
                live = mask[5 * k + 4 : 5 * k + 5, 0:1]
                for r in range(2):
                    here = slice(r * rows + k * SEQ, r * rows + (k + 1) * SEQ)
                    col = (2 * i + r) * C + at_c
                    mix[part, k, pl.ds(r, SEQ, stride=2), :] = (
                        product[here, 128 * part : 128 * (part + 1)]
                        + acc[here, 128 * at : 128 * (at + 1)]
                        + feat[2, k * SEQ : (k + 1) * SEQ, col : col + 128]
                        + both_bias[:, at_c : at_c + 128]
                    ) * live
                out[k, i, :, at_c : at_c + 128] = mix[part, k].astype(BF16)

    for copy in share_copies + stat_copies + tok_copies:
        copy.wait_send()
    sent = sendbuf.at[pl.ds(0, SEQ - 1)]
    pltpu.make_async_copy(sent, sent, out_send).wait()


def shards(
    hidden,
    modulation,
    projection,
    projection_bias,
    input_kernel,
    input_bias,
    norm_gain,
    block_kernel,
    block_bias,
    frame_counts,
    decoder_plan,
):
    hbm = pl.BlockSpec(memory_space=pltpu.HBM)
    return pl.pallas_call(
        kernel,
        out_shape=jax.ShapeDtypeStruct((CAP, 2, 2 * SEQ, C), BF16),
        in_specs=[hbm] * 11,
        out_specs=pl.BlockSpec(memory_space=pltpu.VMEM),
        scratch_shapes=[
            pltpu.VMEM((FRAMES, DL), BF16),
            pltpu.VMEM((2, REQ, DL), F32),
            pltpu.VMEM((4 * Z, DL), BF16),
            pltpu.VMEM((1, 4 * Z), F32),
            pltpu.VMEM((1, REQ), jnp.int32),
            pltpu.VMEM((1, FRAMES), jnp.int32),
            pltpu.VMEM((27, Z, C), BF16),
            pltpu.VMEM((C,), F32),
            pltpu.VMEM((C,), F32),
            pltpu.VMEM((C,), F32),
            pltpu.VMEM((2 * ROW, QF), F32),
            pltpu.VMEM((ROW - 1, 2 * ROW, QF), F32),
            pltpu.VMEM((DL, 128), BF16),
            pltpu.VMEM((4 * REQ, DL), BF16),
            pltpu.VMEM((REQ, 128), F32),
            pltpu.VMEM((REQ, 128), BF16),
            pltpu.VMEM((ROW - 1, REQ, 128), BF16),
            pltpu.VMEM((ROW, QF // 2, 128), F32),
            pltpu.VMEM((ROW, QF // 2, 128), F32),
            pltpu.VMEM((ROW, QF // 2, 128), F32),
            pltpu.VMEM((ROW, QF // 2, 128), BF16),
            pltpu.VMEM((ROW - 1, ROW, QF // 2, 128), BF16),
            pltpu.VMEM((2 * FRAMES, 128), BF16),
            pltpu.VMEM((10 * SEQ, 2 * FRAMES), BF16),
            pltpu.VMEM((SEQ, 5, 2, 128), BF16),
            pltpu.VMEM((SEQ, 5, 2, 128), BF16),
            pltpu.VMEM((16, SEQ, 128), BF16),
            pltpu.VMEM((256, 640), BF16),
            pltpu.VMEM((24, 128), F32),
            pltpu.VMEM((3, 6 * C, 2 * C), BF16),
            pltpu.VMEM((24 * Z, 4 * C), BF16),
            pltpu.VMEM((3, 2 * CAP * SEQ, 6 * C), BF16),
            pltpu.VMEM((2 * CAP * SEQ, 2 * C), F32),
            pltpu.VMEM((3, CAP * SEQ, 4 * C), F32),
            pltpu.VMEM((2, CAP, 2 * SEQ, 128), F32),
            pltpu.SemaphoreType.DMA((10 + ROW,)),
            pltpu.SemaphoreType.DMA((ROW - 1,)),
            pltpu.SemaphoreType.DMA((ROW - 1,)),
            pltpu.SemaphoreType.DMA((ROW - 1,)),
            pltpu.SemaphoreType.DMA((ROW - 1,)),
            pltpu.SemaphoreType.DMA((ROW, ROW - 1)),
            pltpu.SemaphoreType.DMA((ROW, ROW - 1)),
            pltpu.SemaphoreType.DMA,
            pltpu.SemaphoreType.DMA,
            pltpu.SemaphoreType.DMA((3,)),
        ],
        compiler_params=pltpu.CompilerParams(
            collective_id=0, has_side_effects=True, vmem_limit_bytes=44 << 20
        ),
    )(*[pltpu.with_memory_space_constraint(x, pltpu.HBM) for x in (
        hidden.reshape(FRAMES, DL),
        modulation,
        projection.T,
        projection_bias.reshape(1, 4 * Z),
        input_kernel,
        input_bias,
        norm_gain,
        block_kernel,
        block_bias,
        frame_counts.reshape(1, REQ),
        decoder_plan.reshape(1, FRAMES),
    )])


def solution(mesh):
    placed = (
        P(None, "seq", "row"),
        P(None, None, "row"),
        P("row", None),
        P(),
        P(),
        P(),
        P(),
        P(),
        P(),
        P(),
        P(),
    )
    return jax.shard_map(
        shards,
        mesh=mesh,
        in_specs=placed,
        out_specs=P(("seq", "row"), None, None, None),
        check_vma=False,
    )
```

```python
import functools

import jax
import jax.numpy as jnp
from jax import lax
from jax.experimental import pallas as pl
from jax.experimental.pallas import tpu as pltpu
from jax.sharding import PartitionSpec as P

MESH = pl.DeviceIdType.MESH
F32 = jnp.float32
BF16 = jnp.bfloat16

D = 5120
DL = 1280
Z = 16
C = 384
CAP = 4
FRAMES = 512
REQ = 64
SEQ = 64
ROW = 4
QF = FRAMES // ROW
EPSILON = 1e-06


def iota(shape, dim):
    return lax.broadcasted_iota(jnp.int32, shape, dim)


def split_bf16(x):
    high = x.astype(BF16)
    return high, (x - high.astype(F32)).astype(BF16)


def dot(a, b):
    return lax.dot_general(a, b, (((1,), (0,)), ((), ())), preferred_element_type=F32)


def dot_nt(a, b):
    return lax.dot_general(a, b, (((1,), (1,)), ((), ())), preferred_element_type=F32)


def to_rows(column, eye):
    return jnp.sum(jnp.where(eye, column, 0.0), axis=0, keepdims=True)


def to_columns(row, eye):
    return jnp.sum(jnp.where(eye, row, 0.0), axis=1, keepdims=True)


def kernel(
    hid_hbm,
    mod_hbm,
    proj_hbm,
    bias_hbm,
    ker1_hbm,
    bias1_hbm,
    gain_hbm,
    ker2_hbm,
    bias2_hbm,
    counts_hbm,
    plan_hbm,
    out,
    hid,
    mod,
    proj,
    bias,
    counts,
    plan,
    ker1,
    bias1,
    gain,
    bias2,
    stats,
    stats_in,
    weight,
    gains,
    share,
    share_out,
    share_in,
    base,
    scale,
    tok,
    tok_out,
    tok_in,
    spread,
    onehot,
    sendbuf,
    recv,
    y,
    mover,
    mask,
    taps,
    w1,
    lhs,
    acc,
    feat,
    mix,
    local_sem,
    stat_send,
    stat_recv,
    share_send,
    share_recv,
    tok_send,
    tok_recv,
    out_send,
    out_recv,
    tap_sem,
):
    my_seq = lax.axis_index("seq")
    my_row = lax.axis_index("row")

    loads = [
        pltpu.make_async_copy(counts_hbm, counts, local_sem.at[0]),
        pltpu.make_async_copy(plan_hbm, plan, local_sem.at[1]),
        pltpu.make_async_copy(proj_hbm, proj, local_sem.at[2]),
        pltpu.make_async_copy(mod_hbm.at[:, 1, :], mod.at[1], local_sem.at[3]),
        pltpu.make_async_copy(mod_hbm.at[:, 0, :], mod.at[0], local_sem.at[13]),
        pltpu.make_async_copy(bias_hbm, bias, local_sem.at[4]),
        pltpu.make_async_copy(ker1_hbm, ker1, local_sem.at[5]),
        pltpu.make_async_copy(bias1_hbm, bias1, local_sem.at[6]),
        pltpu.make_async_copy(gain_hbm, gain, local_sem.at[7]),
        pltpu.make_async_copy(bias2_hbm, bias2, local_sem.at[8]),
    ]
    hid_loads = [
        pltpu.make_async_copy(
            hid_hbm.at[pl.ds(QF * q, QF)], hid.at[pl.ds(QF * q, QF)], local_sem.at[9 + q]
        )
        for q in range(ROW)
    ]
    for copy in [loads[3], loads[4], loads[2]] + hid_loads + loads[0:2] + [loads[5]]:
        copy.start()

    barrier = pltpu.get_barrier_semaphore()
    for i in range(1, ROW):
        pl.semaphore_signal(
            barrier,
            inc=1,
            device_id=(my_seq, lax.rem(my_row + i, ROW)),
            device_id_type=MESH,
        )

    my_y, my_z, my_core = my_seq // 16, lax.rem(my_seq, 16) // 2, lax.rem(my_seq, 2)
    lines = [
        lax.rem(my_y + y, 4) * 16 + lax.rem(my_core + core, 2) for y in (2, 3, 1, 0) for core in (1, 0)
    ]

    def every_other(act):
        def along(j, carry):
            step = (j + 1) // 2
            to_z = lax.rem(my_z + 4 + step * (2 * lax.rem(j, 2) - 1), 8) * 2
            for line in lines:
                act(line + to_z)
            return carry

        lax.fori_loop(0, 7, along, 0)
        for line in lines[:-1]:
            act(line + my_z * 2)

    def greet(to):
        pl.semaphore_signal(barrier, inc=1, device_id=(to, my_row), device_id_type=MESH)

    every_other(greet)

    eye = iota((QF, QF), 0) == iota((QF, QF), 1)

    for copy in loads[0:2]:
        copy.wait()
    counts_row = counts[...].astype(F32)
    square = (REQ, REQ)
    counts_col = jnp.sum(
        jnp.where(iota(square, 0) == iota(square, 1), counts_row, 0.0), axis=1, keepdims=True
    )
    ends_col = jnp.sum(
        jnp.where(iota(square, 1) <= iota(square, 0), counts_row, 0.0), axis=1, keepdims=True
    )
    starts_col = ends_col - counts_col
    wide = (REQ, 2 * REQ)
    request_lane = lax.rem(iota(wide, 1), REQ)
    ends_row = jnp.sum(
        jnp.where(iota(wide, 0) <= request_lane, counts_col, 0.0), axis=0, keepdims=True
    )
    starts_row = jnp.sum(
        jnp.where(iota(wide, 0) < request_lane, counts_col, 0.0), axis=0, keepdims=True
    )

    for copy in loads[2:6]:
        copy.wait()

    lanes = (Z * 4, 2 * Z * 4)
    lane = lax.rem(iota(lanes, 1), 4 * Z)
    wanted = lax.rem(lane // Z, 2) * (2 * Z) + (lane // (2 * Z)) * Z + lax.rem(lane, Z)
    reorder = jnp.where(iota(lanes, 0) == wanted, 1.0, 0.0).astype(BF16)
    weight[...] = lax.dot_general(
        proj[...], reorder, (((0,), (0,)), ((), ())), preferred_element_type=F32
    ).astype(BF16)
    bias_hi, bias_lo = split_bf16(jnp.broadcast_to(bias[...], (16, 4 * Z)))
    bias_lo2 = (
        jnp.broadcast_to(bias[...], (16, 4 * Z)) - bias_hi.astype(F32) - bias_lo.astype(F32)
    ).astype(BF16)
    bias_row = (dot(bias_hi, reorder) + dot(bias_lo, reorder) + dot(bias_lo2, reorder))[0:1, :]

    gains[0:REQ, :], gains[REQ : 2 * REQ, :] = split_bf16(1.0 + mod[1])
    gains[2 * REQ : 3 * REQ, :], gains[3 * REQ : 4 * REQ, :] = split_bf16(mod[0])
    by_part = dot(gains[...], weight[...])
    gain_weight = by_part[0:REQ] + by_part[REQ : 2 * REQ]
    shift_weight = by_part[2 * REQ : 3 * REQ] + by_part[3 * REQ : 4 * REQ]
    share[...] = jnp.where(iota((REQ, 128), 1) < 64, gain_weight, shift_weight)
    share_out[...] = share[...].astype(BF16)

    members = []
    for q in range(ROW):
        frame = (iota((QF, 2 * REQ), 0) + QF * q).astype(F32)
        members.append(
            jnp.where(
                jnp.logical_and(frame >= starts_row, frame < ends_row), 1.0, 0.0
            ).astype(BF16)
        )

    share_copies, stat_copies, tok_copies = [], [], []

    def to_row_peers(source, target, send_sem, recv_sem, copies):
        for i in (2, 1, 3):
            copy = pltpu.make_async_remote_copy(
                src_ref=source,
                dst_ref=target(i - 1),
                send_sem=send_sem(i - 1),
                recv_sem=recv_sem(i - 1),
                device_id=(my_seq, lax.rem(my_row + i, ROW)),
                device_id_type=MESH,
            )
            copy.start()
            copies.append(copy)

    def send_quarter(q):
        to_row_peers(
            tok_out.at[q],
            lambda n: tok_in.at[n, q],
            lambda n: tok_send.at[q, n],
            lambda n: tok_recv.at[q, n],
            tok_copies,
        )

    half = iota((QF // 2, 128), 1) < 64
    share_rows = jnp.concatenate(split_bf16(gain_weight), axis=0)
    means = []
    for q in range(ROW):
        hid_loads[q].wait()
        h = hid[QF * q : QF * (q + 1), :].astype(F32)
        one = jnp.sum(h, axis=1, keepdims=True)
        two = jnp.sum(h * h, axis=1, keepdims=True)
        means.append(one / DL)
        stats[q : q + 1, :] = to_rows(one, eye)
        stats[ROW + q : ROW + q + 1, :] = to_rows(two, eye)

    def project(q):
        h = hid[QF * q : QF * (q + 1), :].astype(F32)
        x_hi, x_lo = split_bf16(h * dot(members[q], gains[0 : 2 * REQ, :]))
        both = dot(jnp.concatenate([x_hi, x_lo], axis=0), weight[...])
        projected = both[0:QF] + both[QF : 2 * QF] - means[q] * dot(members[q], share_rows)
        tok[q] = jnp.where(half, projected[0 : QF // 2], projected[QF // 2 : QF])
        tok_out[q] = tok[q].astype(BF16)

    pl.semaphore_wait(barrier, ROW - 1 + SEQ - 1)
    to_row_peers(
        share_out,
        lambda n: share_in.at[n],
        lambda n: share_send.at[n],
        lambda n: share_recv.at[n],
        share_copies,
    )
    to_row_peers(
        stats,
        lambda n: stats_in.at[n],
        lambda n: stat_send.at[n],
        lambda n: stat_recv.at[n],
        stat_copies,
    )
    project(0)
    send_quarter(0)
    project(1)
    send_quarter(1)
    project(2)
    send_quarter(2)
    project(3)
    send_quarter(3)

    for copy in loads[6:]:
        copy.start()
    for t in range(3):
        for p in range(2):
            for e in range(3):
                for i in range(2):
                    pltpu.make_async_copy(
                        ker2_hbm.at[9 * t + 3 * (p - i + 1) + e],
                        taps.at[t, pl.ds((3 * p + e) * C, C), pl.ds(i * C, C)],
                        tap_sem.at[t],
                    ).start()


    plan_row = plan[...]
    plan_f32 = plan_row.astype(F32)
    frame_row = iota((1, FRAMES), 1)
    frame_f32 = frame_row.astype(F32)
    rank = jnp.zeros((1, FRAMES), F32)
    for q in range(ROW):
        plan_col = to_columns(plan_f32[:, QF * q : QF * (q + 1)], eye)
        before = iota((QF, FRAMES), 0) + QF * q < iota((QF, FRAMES), 1)
        rank += jnp.sum(
            jnp.where(jnp.logical_and(plan_col == plan_f32, before), 1.0, 0.0),
            axis=0,
            keepdims=True,
        )
    code = jnp.where(
        plan_row - (plan_row // ROW) * ROW == my_row,
        (plan_row // ROW).astype(F32) * CAP + rank,
        -1.0,
    )
    by_request = (REQ, FRAMES)
    frame_of = iota(by_request, 1).astype(F32)
    first = jnp.sum(
        jnp.where(
            jnp.logical_and(frame_of >= starts_col, frame_of < ends_col), starts_col, 0.0
        ),
        axis=0,
        keepdims=True,
    )
    shifted = []
    for back in range(5):
        if back == 0:
            shifted.append(code)
            continue
        code_ahead = pltpu.roll(jnp.broadcast_to(code, (8, FRAMES)), FRAMES - back, 1)[0:1]
        first_ahead = pltpu.roll(jnp.broadcast_to(first, (8, FRAMES)), FRAMES - back, 1)[0:1]
        shifted.append(
            jnp.where(
                jnp.logical_and(first_ahead <= frame_f32, frame_row < FRAMES - back),
                code_ahead,
                -1.0,
            )
        )

    def wanted_by(rows, halves):
        latent_row = halves - (halves // 5) * 5
        picked = jnp.broadcast_to(shifted[0], (rows, FRAMES))
        for back in range(1, 5):
            picked = jnp.where(latent_row == 4 - back, shifted[back], picked)
        return picked - (halves // 5).astype(F32)

    own = wanted_by(24, iota((24, FRAMES), 0))
    mask[...] = jnp.broadcast_to(
        jnp.sum(jnp.where(own == (my_seq * CAP).astype(F32), 1.0, 0.0), axis=1, keepdims=True),
        (24, 128),
    )
    rows = iota((80, FRAMES), 0)
    table = jnp.concatenate(
        [
            wanted_by(80, 2 * lax.rem(rows, 10) + high) - (rows // 10 * CAP).astype(F32)
            for high in range(2)
        ],
        axis=1,
    )
    for n in range(SEQ // 8):
        onehot[80 * n : 80 * (n + 1), :] = jnp.where(table == float(8 * CAP * n), 1.0, 0.0).astype(
            BF16
        )

    for copy in share_copies + stat_copies:
        copy.wait_recv()
    total = stats[...] + stats_in[0] + stats_in[1] + stats_in[2]
    average_row = total[0:ROW] / D
    inverse_row = lax.rsqrt(total[ROW : 2 * ROW] / D - average_row * average_row + EPSILON)
    shares = [share[...]] + [share_in[n].astype(F32) for n in range(ROW - 1)]
    left_half = iota((REQ, 128), 1) < 64
    shift_total = shares[0] + shares[1] + shares[2] + shares[3]
    spreads = [jnp.where(left_half, v, pltpu.roll(v, 64, 1)) for v in shares]
    spreads.append(jnp.where(left_half, pltpu.roll(shift_total, 64, 1), shift_total))
    spreads = jnp.concatenate(split_bf16(jnp.concatenate(spreads, axis=1)), axis=0)
    sums = [stats, stats_in.at[0], stats_in.at[1], stats_in.at[2]]
    for q in range(ROW):
        by_frame = dot(members[q], spreads)
        inverse = to_columns(inverse_row[q : q + 1], eye)
        rest = by_frame[:, 512:640] + bias_row
        for n in range(ROW):
            offset = (sums[n][q : q + 1, :] / DL - average_row[q : q + 1]) * inverse_row[q : q + 1]
            rest += to_columns(offset, eye) * by_frame[:, 128 * n : 128 * (n + 1)]
        base[q] = jnp.where(half, rest[0 : QF // 2], rest[QF // 2 : QF])
        scale[q] = jnp.where(half, inverse[0 : QF // 2], inverse[QF // 2 : QF])

    for copy in loads[6:]:
        copy.wait()

    def fill(start, a, columns):
        for n, (position, q) in enumerate(columns):
            for i in range(2):
                for r in range(2):
                    e = position - r + 1
                    if 0 <= e <= 2:
                        block = ker1[9 * a + 3 * (q - i + 1) + e]
                    else:
                        block = jnp.zeros((Z, C), BF16)
                    w1[start + Z * n : start + Z * (n + 1), (2 * i + r) * C : (2 * i + r + 1) * C] = (
                        block
                    )

    own = [(0, 0), (0, 1), (1, 0), (1, 1)]
    rim = [(2, 0), (2, 1), (-1, 0), (-1, 1)]
    for start, a, columns in (
        (0, 0, own),
        (64, 1, own),
        (128, 0, rim),
        (192, 2, own),
        (256, 1, rim),
        (320, 2, rim),
    ):
        fill(start, a, columns)

    moved = (256, 640)
    to_row, from_row = iota(moved, 0), iota(moved, 1)
    group, place = to_row // 16, lax.rem(to_row, 16) * 10
    low = lax.rem(group, 4) * 5 + group // 4
    high = low + 1
    mover[...] = jnp.where(
        jnp.logical_or(
            from_row == lax.rem(low, 2) * 160 + place + low // 2,
            from_row == (2 + lax.rem(high, 2)) * 160 + place + high // 2,
        ),
        1.0,
        0.0,
    ).astype(BF16)

    bias1_row = bias1[...].reshape(1, C)
    gain_row = gain[...].reshape(1, C)

    def latents(q):
        for copy in tok_copies[(ROW - 1) * q : (ROW - 1) * (q + 1)]:
            copy.wait_recv()
        here = (
            (
                (
                    tok[q]
                    + tok_in[0, q].astype(F32)
                    + tok_in[1, q].astype(F32)
                    + tok_in[2, q].astype(F32)
                )
                * scale[q]
                + base[q]
            )
            .astype(BF16)
            .astype(F32)
        )
        there = pltpu.roll(here, 64, 1)
        low, high = jnp.where(half, here, 0.0), jnp.where(half, 0.0, here)
        low_moved, high_moved = jnp.where(half, there, 0.0), jnp.where(half, 0.0, there)
        for at, block in (
            (QF * q, low),
            (QF * q + 64, low_moved),
            (FRAMES + QF * q, high_moved),
            (FRAMES + QF * q + 64, high),
        ):
            spread[at : at + 64, :] = block.astype(BF16)
    def gathered(rows, first, last):
        low, high = slice(QF * first, QF * last), slice(FRAMES + QF * first, FRAMES + QF * last)
        return dot(onehot[rows, low], spread[low, :]) + dot(onehot[rows, high], spread[high, :])

    for q in range(ROW - 1):
        latents(q)
    found = [
        gathered(slice(160 * block, 160 * (block + 1)), 0, ROW - 1) for block in range(4)
    ]
    latents(ROW - 1)
    for block in range(4):
        sendbuf[16 * block : 16 * (block + 1)] = (
            (found[block] + gathered(slice(160 * block, 160 * (block + 1)), ROW - 1, ROW))
            .astype(BF16)
            .reshape(16, 5, 2, 128)
        )

    def post(to):
        pltpu.make_async_remote_copy(
            src_ref=sendbuf.at[to],
            dst_ref=recv.at[my_seq],
            send_sem=out_send,
            recv_sem=out_recv,
            device_id=(to, my_row),
            device_id_type=MESH,
        ).start()

    every_other(post)
    recv[my_seq] = sendbuf[my_seq]

    for t in range(3):
        pltpu.make_async_copy(taps.at[t], taps.at[t], tap_sem.at[t]).wait()
    arrived = recv.at[pl.ds(0, SEQ - 1)]
    pltpu.make_async_copy(arrived, arrived, out_recv).wait()
    left = iota((160, 128), 1) < 64
    for block in range(4):
        got = recv[16 * block : 16 * (block + 1)].reshape(160, 128).astype(F32)
        turned = pltpu.roll(got, 64, 1)
        parts = jnp.concatenate(
            [
                jnp.where(left, got, 0.0),
                jnp.where(left, turned, 0.0),
                jnp.where(left, 0.0, turned),
                jnp.where(left, 0.0, got),
            ],
            axis=0,
        ).astype(BF16)
        y[:, 16 * block : 16 * (block + 1), :] = (
            dot(mover[...], parts).astype(BF16).reshape(16, 16, 128)
        )

    rows = CAP * SEQ
    column = lax.rem(iota((rows, 128), 0), SEQ)
    lane = iota((rows, 128), 1)

    def rims(v):
        right = jnp.where(column == SEQ - 1, 0.0, pltpu.roll(v, rows - 1, 0))
        left = jnp.where(column == 0, 0.0, pltpu.roll(v, 1, 0))
        return jnp.where(lax.rem(lane, 64) < 32, right, left)

    wide = [y[CAP * t : CAP * (t + 1)].reshape(rows, 128).astype(F32) for t in range(4)]
    around = [rims(v) for v in wide]
    first_col = iota((SEQ, C), 0) == 0
    last_col = iota((SEQ, C), 0) == SEQ - 1
    xs = []
    for t in range(3):
        xs.append(
            jnp.concatenate(
                [wide[t], jnp.where(lane < 64, around[t], wide[t + 1]), around[t + 1]], axis=1
            ).astype(BF16)
        )

    def features(t):
        for p in range(2):
            cols = slice(2 * p * C, 2 * (p + 1) * C)
            feat[t, :, cols] = dot(xs[t], w1[:, cols])

    def activate(t):
        for k in range(CAP):
            live = 0.5 * mask[5 * k + t + 2 : 5 * k + t + 3, 0:1]
            here = slice(k * SEQ, (k + 1) * SEQ)
            for p in range(2):
                for r in range(2):
                    v = feat[t, here, (2 * p + r) * C : (2 * p + r + 1) * C] + bias1_row
                    factor = lax.rsqrt(jnp.mean(v * v, axis=1, keepdims=True) + EPSILON) * live
                    n = v * factor * gain_row
                    a = n + n * jnp.tanh(n)

                    def put(side, e, value):
                        lhs[
                            t,
                            side * rows + k * SEQ : side * rows + (k + 1) * SEQ,
                            (3 * p + e) * C : (3 * p + e + 1) * C,
                        ] = value.astype(BF16)

                    if r == 0:
                        put(0, 1, a)
                        put(1, 0, a)
                        put(1, 2, jnp.where(last_col, 0.0, pltpu.roll(a, SEQ - 1, 0)))
                    else:
                        put(0, 2, a)
                        put(1, 1, a)
                        put(0, 0, jnp.where(first_col, 0.0, pltpu.roll(a, 1, 0)))

    features(0)
    activate(0)
    for t in range(2):
        features(t + 1)
        product = dot(lhs[t], taps[t])
        if t == 0:
            acc[...] = product
        else:
            acc[...] += product
        activate(t + 1)

    both_bias = bias2[...].reshape(1, C) + bias1_row
    for n in range(3):
        product = dot(lhs[2], taps[2, :, 256 * n : 256 * (n + 1)])
        for part in range(2):
            at = 2 * n + part
            i, at_c = at // 3, 128 * (at % 3)
            for k in range(CAP):
                live = mask[5 * k + 4 : 5 * k + 5, 0:1]
                for r in range(2):
                    here = slice(r * rows + k * SEQ, r * rows + (k + 1) * SEQ)
                    col = (2 * i + r) * C + at_c
                    mix[part, k, pl.ds(r, SEQ, stride=2), :] = (
                        product[here, 128 * part : 128 * (part + 1)]
                        + acc[here, 128 * at : 128 * (at + 1)]
                        + feat[2, k * SEQ : (k + 1) * SEQ, col : col + 128]
                        + both_bias[:, at_c : at_c + 128]
                    ) * live
                out[k, i, :, at_c : at_c + 128] = mix[part, k].astype(BF16)

    for copy in share_copies + stat_copies + tok_copies:
        copy.wait_send()
    sent = sendbuf.at[pl.ds(0, SEQ - 1)]
    pltpu.make_async_copy(sent, sent, out_send).wait()


def shards(
    hidden,
    modulation,
    projection,
    projection_bias,
    input_kernel,
    input_bias,
    norm_gain,
    block_kernel,
    block_bias,
    frame_counts,
    decoder_plan,
):
    hbm = pl.BlockSpec(memory_space=pltpu.HBM)
    return pl.pallas_call(
        kernel,
        out_shape=jax.ShapeDtypeStruct((CAP, 2, 2 * SEQ, C), BF16),
        in_specs=[hbm] * 11,
        out_specs=pl.BlockSpec(memory_space=pltpu.VMEM),
        scratch_shapes=[
            pltpu.VMEM((FRAMES, DL), BF16),
            pltpu.VMEM((2, REQ, DL), F32),
            pltpu.VMEM((4 * Z, DL), BF16),
            pltpu.VMEM((1, 4 * Z), F32),
            pltpu.VMEM((1, REQ), jnp.int32),
            pltpu.VMEM((1, FRAMES), jnp.int32),
            pltpu.VMEM((27, Z, C), BF16),
            pltpu.VMEM((C,), F32),
            pltpu.VMEM((C,), F32),
            pltpu.VMEM((C,), F32),
            pltpu.VMEM((2 * ROW, QF), F32),
            pltpu.VMEM((ROW - 1, 2 * ROW, QF), F32),
            pltpu.VMEM((DL, 128), BF16),
            pltpu.VMEM((4 * REQ, DL), BF16),
            pltpu.VMEM((REQ, 128), F32),
            pltpu.VMEM((REQ, 128), BF16),
            pltpu.VMEM((ROW - 1, REQ, 128), BF16),
            pltpu.VMEM((ROW, QF // 2, 128), F32),
            pltpu.VMEM((ROW, QF // 2, 128), F32),
            pltpu.VMEM((ROW, QF // 2, 128), F32),
            pltpu.VMEM((ROW, QF // 2, 128), BF16),
            pltpu.VMEM((ROW - 1, ROW, QF // 2, 128), BF16),
            pltpu.VMEM((2 * FRAMES, 128), BF16),
            pltpu.VMEM((10 * SEQ, 2 * FRAMES), BF16),
            pltpu.VMEM((SEQ, 5, 2, 128), BF16),
            pltpu.VMEM((SEQ, 5, 2, 128), BF16),
            pltpu.VMEM((16, SEQ, 128), BF16),
            pltpu.VMEM((256, 640), BF16),
            pltpu.VMEM((24, 128), F32),
            pltpu.VMEM((3, 6 * C, 2 * C), BF16),
            pltpu.VMEM((24 * Z, 4 * C), BF16),
            pltpu.VMEM((3, 2 * CAP * SEQ, 6 * C), BF16),
            pltpu.VMEM((2 * CAP * SEQ, 2 * C), F32),
            pltpu.VMEM((3, CAP * SEQ, 4 * C), F32),
            pltpu.VMEM((2, CAP, 2 * SEQ, 128), F32),
            pltpu.SemaphoreType.DMA((10 + ROW,)),
            pltpu.SemaphoreType.DMA((ROW - 1,)),
            pltpu.SemaphoreType.DMA((ROW - 1,)),
            pltpu.SemaphoreType.DMA((ROW - 1,)),
            pltpu.SemaphoreType.DMA((ROW - 1,)),
            pltpu.SemaphoreType.DMA((ROW, ROW - 1)),
            pltpu.SemaphoreType.DMA((ROW, ROW - 1)),
            pltpu.SemaphoreType.DMA,
            pltpu.SemaphoreType.DMA,
            pltpu.SemaphoreType.DMA((3,)),
        ],
        compiler_params=pltpu.CompilerParams(
            collective_id=0, has_side_effects=True, vmem_limit_bytes=44 << 20
        ),
    )(*[pltpu.with_memory_space_constraint(x, pltpu.HBM) for x in (
        hidden.reshape(FRAMES, DL),
        modulation,
        projection.T,
        projection_bias.reshape(1, 4 * Z),
        input_kernel,
        input_bias,
        norm_gain,
        block_kernel,
        block_bias,
        frame_counts.reshape(1, REQ),
        decoder_plan.reshape(1, FRAMES),
    )])


def solution(mesh):
    placed = (
        P(None, "seq", "row"),
        P(None, None, "row"),
        P("row", None),
        P(),
        P(),
        P(),
        P(),
        P(),
        P(),
        P(),
        P(),
    )
    return jax.shard_map(
        shards,
        mesh=mesh,
        in_specs=placed,
        out_specs=P(("seq", "row"), None, None, None),
        check_vma=False,
    )
```

```python
import functools

import jax
import jax.numpy as jnp
from jax import lax
from jax.experimental import pallas as pl
from jax.experimental.pallas import tpu as pltpu
from jax.sharding import PartitionSpec as P

MESH = pl.DeviceIdType.MESH
F32 = jnp.float32
BF16 = jnp.bfloat16

D = 5120
DL = 1280
Z = 16
C = 384
CAP = 4
FRAMES = 512
REQ = 64
SEQ = 64
ROW = 4
QF = FRAMES // ROW
EPSILON = 1e-06


def iota(shape, dim):
    return lax.broadcasted_iota(jnp.int32, shape, dim)


def split_bf16(x):
    high = x.astype(BF16)
    return high, (x - high.astype(F32)).astype(BF16)


def dot(a, b):
    return lax.dot_general(a, b, (((1,), (0,)), ((), ())), preferred_element_type=F32)


def dot_nt(a, b):
    return lax.dot_general(a, b, (((1,), (1,)), ((), ())), preferred_element_type=F32)


def to_rows(column, eye):
    return jnp.sum(jnp.where(eye, column, 0.0), axis=0, keepdims=True)


def to_columns(row, eye):
    return jnp.sum(jnp.where(eye, row, 0.0), axis=1, keepdims=True)


def kernel(
    hid_hbm,
    mod_hbm,
    proj_hbm,
    bias_hbm,
    ker1_hbm,
    bias1_hbm,
    gain_hbm,
    ker2_hbm,
    bias2_hbm,
    counts_hbm,
    plan_hbm,
    out,
    hid,
    mod,
    proj,
    bias,
    counts,
    plan,
    ker1,
    bias1,
    gain,
    bias2,
    stats,
    stats_in,
    weight,
    gains,
    share,
    share_out,
    share_in,
    base,
    scale,
    tok,
    tok_out,
    tok_in,
    spread,
    onehot,
    sendbuf,
    recv,
    y,
    mover,
    mask,
    taps,
    w1,
    lhs,
    acc,
    feat,
    mix,
    local_sem,
    stat_send,
    stat_recv,
    share_send,
    share_recv,
    tok_send,
    tok_recv,
    out_send,
    out_recv,
    tap_sem,
):
    my_seq = lax.axis_index("seq")
    my_row = lax.axis_index("row")

    loads = [
        pltpu.make_async_copy(counts_hbm, counts, local_sem.at[0]),
        pltpu.make_async_copy(plan_hbm, plan, local_sem.at[1]),
        pltpu.make_async_copy(proj_hbm, proj, local_sem.at[2]),
        pltpu.make_async_copy(mod_hbm.at[:, 1, :], mod.at[1], local_sem.at[3]),
        pltpu.make_async_copy(mod_hbm.at[:, 0, :], mod.at[0], local_sem.at[13]),
        pltpu.make_async_copy(bias_hbm, bias, local_sem.at[4]),
        pltpu.make_async_copy(ker1_hbm, ker1, local_sem.at[5]),
        pltpu.make_async_copy(bias1_hbm, bias1, local_sem.at[6]),
        pltpu.make_async_copy(gain_hbm, gain, local_sem.at[7]),
        pltpu.make_async_copy(bias2_hbm, bias2, local_sem.at[8]),
    ]
    hid_loads = [
        pltpu.make_async_copy(
            hid_hbm.at[pl.ds(QF * q, QF)], hid.at[pl.ds(QF * q, QF)], local_sem.at[9 + q]
        )
        for q in range(ROW)
    ]
    for copy in [loads[3], loads[4], loads[2]] + hid_loads + loads[0:2] + [loads[5]]:
        copy.start()

    barrier = pltpu.get_barrier_semaphore()
    for i in range(1, ROW):
        pl.semaphore_signal(
            barrier,
            inc=1,
            device_id=(my_seq, lax.rem(my_row + i, ROW)),
            device_id_type=MESH,
        )

    my_y, my_z, my_core = my_seq // 16, lax.rem(my_seq, 16) // 2, lax.rem(my_seq, 2)
    lines = [
        lax.rem(my_y + y, 4) * 16 + lax.rem(my_core + core, 2) for y in (2, 3, 1, 0) for core in (1, 0)
    ]

    def every_other(act):
        def along(j, carry):
            step = (j + 1) // 2
            to_z = lax.rem(my_z + 4 + step * (2 * lax.rem(j, 2) - 1), 8) * 2
            for line in lines:
                act(line + to_z)
            return carry

        lax.fori_loop(0, 7, along, 0)
        for line in lines[:-1]:
            act(line + my_z * 2)

    def greet(to):
        pl.semaphore_signal(barrier, inc=1, device_id=(to, my_row), device_id_type=MESH)

    every_other(greet)

    eye = iota((QF, QF), 0) == iota((QF, QF), 1)

    for copy in loads[0:2]:
        copy.wait()
    counts_row = counts[...].astype(F32)
    square = (REQ, REQ)
    counts_col = jnp.sum(
        jnp.where(iota(square, 0) == iota(square, 1), counts_row, 0.0), axis=1, keepdims=True
    )
    ends_col = jnp.sum(
        jnp.where(iota(square, 1) <= iota(square, 0), counts_row, 0.0), axis=1, keepdims=True
    )
    starts_col = ends_col - counts_col
    wide = (REQ, 2 * REQ)
    request_lane = lax.rem(iota(wide, 1), REQ)
    ends_row = jnp.sum(
        jnp.where(iota(wide, 0) <= request_lane, counts_col, 0.0), axis=0, keepdims=True
    )
    starts_row = jnp.sum(
        jnp.where(iota(wide, 0) < request_lane, counts_col, 0.0), axis=0, keepdims=True
    )

    for copy in loads[2:6]:
        copy.wait()

    lanes = (Z * 4, 2 * Z * 4)
    lane = lax.rem(iota(lanes, 1), 4 * Z)
    wanted = lax.rem(lane // Z, 2) * (2 * Z) + (lane // (2 * Z)) * Z + lax.rem(lane, Z)
    reorder = jnp.where(iota(lanes, 0) == wanted, 1.0, 0.0).astype(BF16)
    weight[...] = lax.dot_general(
        proj[...], reorder, (((0,), (0,)), ((), ())), preferred_element_type=F32
    ).astype(BF16)
    bias_hi, bias_lo = split_bf16(jnp.broadcast_to(bias[...], (16, 4 * Z)))
    bias_lo2 = (
        jnp.broadcast_to(bias[...], (16, 4 * Z)) - bias_hi.astype(F32) - bias_lo.astype(F32)
    ).astype(BF16)
    bias_row = (dot(bias_hi, reorder) + dot(bias_lo, reorder) + dot(bias_lo2, reorder))[0:1, :]

    gains[0:REQ, :], gains[REQ : 2 * REQ, :] = split_bf16(1.0 + mod[1])
    gains[2 * REQ : 3 * REQ, :], gains[3 * REQ : 4 * REQ, :] = split_bf16(mod[0])
    by_part = dot(gains[...], weight[...])
    gain_weight = by_part[0:REQ] + by_part[REQ : 2 * REQ]
    shift_weight = by_part[2 * REQ : 3 * REQ] + by_part[3 * REQ : 4 * REQ]
    share[...] = jnp.where(iota((REQ, 128), 1) < 64, gain_weight, shift_weight)
    share_out[...] = share[...].astype(BF16)

    members = []
    for q in range(ROW):
        frame = (iota((QF, 2 * REQ), 0) + QF * q).astype(F32)
        members.append(
            jnp.where(
                jnp.logical_and(frame >= starts_row, frame < ends_row), 1.0, 0.0
            ).astype(BF16)
        )

    share_copies, stat_copies, tok_copies = [], [], []

    def to_row_peers(source, target, send_sem, recv_sem, copies):
        for i in (2, 1, 3):
            copy = pltpu.make_async_remote_copy(
                src_ref=source,
                dst_ref=target(i - 1),
                send_sem=send_sem(i - 1),
                recv_sem=recv_sem(i - 1),
                device_id=(my_seq, lax.rem(my_row + i, ROW)),
                device_id_type=MESH,
            )
            copy.start()
            copies.append(copy)

    def send_quarter(q):
        to_row_peers(
            tok_out.at[q],
            lambda n: tok_in.at[n, q],
            lambda n: tok_send.at[q, n],
            lambda n: tok_recv.at[q, n],
            tok_copies,
        )

    half = iota((QF // 2, 128), 1) < 64
    share_rows = jnp.concatenate(split_bf16(gain_weight), axis=0)
    means = []
    for q in range(ROW):
        hid_loads[q].wait()
        h = hid[QF * q : QF * (q + 1), :].astype(F32)
        one = jnp.sum(h, axis=1, keepdims=True)
        two = jnp.sum(h * h, axis=1, keepdims=True)
        means.append(one / DL)
        stats[q : q + 1, :] = to_rows(one, eye)
        stats[ROW + q : ROW + q + 1, :] = to_rows(two, eye)

    def project(q):
        h = hid[QF * q : QF * (q + 1), :].astype(F32)
        x_hi, x_lo = split_bf16(h * dot(members[q], gains[0 : 2 * REQ, :]))
        both = dot(jnp.concatenate([x_hi, x_lo], axis=0), weight[...])
        projected = both[0:QF] + both[QF : 2 * QF] - means[q] * dot(members[q], share_rows)
        tok[q] = jnp.where(half, projected[0 : QF // 2], projected[QF // 2 : QF])
        tok_out[q] = tok[q].astype(BF16)

    pl.semaphore_wait(barrier, ROW - 1 + SEQ - 1)
    to_row_peers(
        share_out,
        lambda n: share_in.at[n],
        lambda n: share_send.at[n],
        lambda n: share_recv.at[n],
        share_copies,
    )
    to_row_peers(
        stats,
        lambda n: stats_in.at[n],
        lambda n: stat_send.at[n],
        lambda n: stat_recv.at[n],
        stat_copies,
    )
    project(0)
    send_quarter(0)
    project(1)
    send_quarter(1)
    project(2)
    send_quarter(2)
    project(3)
    send_quarter(3)

    for copy in loads[6:]:
        copy.start()
    for t in range(3):
        for p in range(2):
            for e in range(3):
                for i in range(2):
                    pltpu.make_async_copy(
                        ker2_hbm.at[9 * t + 3 * (p - i + 1) + e],
                        taps.at[t, pl.ds((3 * p + e) * C, C), pl.ds(i * C, C)],
                        tap_sem.at[t],
                    ).start()


    plan_row = plan[...]
    plan_f32 = plan_row.astype(F32)
    frame_row = iota((1, FRAMES), 1)
    frame_f32 = frame_row.astype(F32)
    rank = jnp.zeros((1, FRAMES), F32)
    for q in range(ROW):
        plan_col = to_columns(plan_f32[:, QF * q : QF * (q + 1)], eye)
        before = iota((QF, FRAMES), 0) + QF * q < iota((QF, FRAMES), 1)
        rank += jnp.sum(
            jnp.where(jnp.logical_and(plan_col == plan_f32, before), 1.0, 0.0),
            axis=0,
            keepdims=True,
        )
    code = jnp.where(
        plan_row - (plan_row // ROW) * ROW == my_row,
        (plan_row // ROW).astype(F32) * CAP + rank,
        -1.0,
    )
    by_request = (REQ, FRAMES)
    frame_of = iota(by_request, 1).astype(F32)
    first = jnp.sum(
        jnp.where(
            jnp.logical_and(frame_of >= starts_col, frame_of < ends_col), starts_col, 0.0
        ),
        axis=0,
        keepdims=True,
    )
    shifted = []
    for back in range(5):
        if back == 0:
            shifted.append(code)
            continue
        code_ahead = pltpu.roll(jnp.broadcast_to(code, (8, FRAMES)), FRAMES - back, 1)[0:1]
        first_ahead = pltpu.roll(jnp.broadcast_to(first, (8, FRAMES)), FRAMES - back, 1)[0:1]
        shifted.append(
            jnp.where(
                jnp.logical_and(first_ahead <= frame_f32, frame_row < FRAMES - back),
                code_ahead,
                -1.0,
            )
        )

    def wanted_by(rows, halves):
        latent_row = halves - (halves // 5) * 5
        picked = jnp.broadcast_to(shifted[0], (rows, FRAMES))
        for back in range(1, 5):
            picked = jnp.where(latent_row == 4 - back, shifted[back], picked)
        return picked - (halves // 5).astype(F32)

    own = wanted_by(24, iota((24, FRAMES), 0))
    mask[...] = jnp.broadcast_to(
        jnp.sum(jnp.where(own == (my_seq * CAP).astype(F32), 1.0, 0.0), axis=1, keepdims=True),
        (24, 128),
    )
    rows = iota((80, FRAMES), 0)
    table = jnp.concatenate(
        [
            wanted_by(80, 2 * lax.rem(rows, 10) + high) - (rows // 10 * CAP).astype(F32)
            for high in range(2)
        ],
        axis=1,
    )
    for n in range(SEQ // 8):
        onehot[80 * n : 80 * (n + 1), :] = jnp.where(table == float(8 * CAP * n), 1.0, 0.0).astype(
            BF16
        )

    for copy in share_copies + stat_copies:
        copy.wait_recv()
    total = stats[...] + stats_in[0] + stats_in[1] + stats_in[2]
    average_row = total[0:ROW] / D
    inverse_row = lax.rsqrt(total[ROW : 2 * ROW] / D - average_row * average_row + EPSILON)
    shares = [share[...]] + [share_in[n].astype(F32) for n in range(ROW - 1)]
    left_half = iota((REQ, 128), 1) < 64
    shift_total = shares[0] + shares[1] + shares[2] + shares[3]
    spreads = [jnp.where(left_half, v, pltpu.roll(v, 64, 1)) for v in shares]
    spreads.append(jnp.where(left_half, pltpu.roll(shift_total, 64, 1), shift_total))
    spreads = jnp.concatenate(split_bf16(jnp.concatenate(spreads, axis=1)), axis=0)
    sums = [stats, stats_in.at[0], stats_in.at[1], stats_in.at[2]]
    for q in range(ROW):
        by_frame = dot(members[q], spreads)
        inverse = to_columns(inverse_row[q : q + 1], eye)
        rest = by_frame[:, 512:640] + bias_row
        for n in range(ROW):
            offset = (sums[n][q : q + 1, :] / DL - average_row[q : q + 1]) * inverse_row[q : q + 1]
            rest += to_columns(offset, eye) * by_frame[:, 128 * n : 128 * (n + 1)]
        base[q] = jnp.where(half, rest[0 : QF // 2], rest[QF // 2 : QF])
        scale[q] = jnp.where(half, inverse[0 : QF // 2], inverse[QF // 2 : QF])

    for copy in loads[6:]:
        copy.wait()

    def fill(start, a, columns):
        for n, (position, q) in enumerate(columns):
            for i in range(2):
                for r in range(2):
                    e = position - r + 1
                    if 0 <= e <= 2:
                        block = ker1[9 * a + 3 * (q - i + 1) + e]
                    else:
                        block = jnp.zeros((Z, C), BF16)
                    w1[start + Z * n : start + Z * (n + 1), (2 * i + r) * C : (2 * i + r + 1) * C] = (
                        block
                    )

    own = [(0, 0), (0, 1), (1, 0), (1, 1)]
    rim = [(2, 0), (2, 1), (-1, 0), (-1, 1)]
    for start, a, columns in (
        (0, 0, own),
        (64, 1, own),
        (128, 0, rim),
        (192, 2, own),
        (256, 1, rim),
        (320, 2, rim),
    ):
        fill(start, a, columns)

    moved = (256, 640)
    to_row, from_row = iota(moved, 0), iota(moved, 1)
    group, place = to_row // 16, lax.rem(to_row, 16) * 10
    low = lax.rem(group, 4) * 5 + group // 4
    high = low + 1
    mover[...] = jnp.where(
        jnp.logical_or(
            from_row == lax.rem(low, 2) * 160 + place + low // 2,
            from_row == (2 + lax.rem(high, 2)) * 160 + place + high // 2,
        ),
        1.0,
        0.0,
    ).astype(BF16)

    bias1_row = bias1[...].reshape(1, C)
    gain_row = gain[...].reshape(1, C)

    def latents(q):
        for copy in tok_copies[(ROW - 1) * q : (ROW - 1) * (q + 1)]:
            copy.wait_recv()
        here = (
            (
                (
                    tok[q]
                    + tok_in[0, q].astype(F32)
                    + tok_in[1, q].astype(F32)
                    + tok_in[2, q].astype(F32)
                )
                * scale[q]
                + base[q]
            )
            .astype(BF16)
            .astype(F32)
        )
        there = pltpu.roll(here, 64, 1)
        low, high = jnp.where(half, here, 0.0), jnp.where(half, 0.0, here)
        low_moved, high_moved = jnp.where(half, there, 0.0), jnp.where(half, 0.0, there)
        for at, block in (
            (QF * q, low),
            (QF * q + 64, low_moved),
            (FRAMES + QF * q, high_moved),
            (FRAMES + QF * q + 64, high),
        ):
            spread[at : at + 64, :] = block.astype(BF16)
    def gathered(rows, first, last):
        low, high = slice(QF * first, QF * last), slice(FRAMES + QF * first, FRAMES + QF * last)
        return dot(onehot[rows, low], spread[low, :]) + dot(onehot[rows, high], spread[high, :])

    for q in range(ROW - 1):
        latents(q)
    found = [
        gathered(slice(160 * block, 160 * (block + 1)), 0, ROW - 1) for block in range(4)
    ]
    latents(ROW - 1)
    for block in range(4):
        sendbuf[16 * block : 16 * (block + 1)] = (
            (found[block] + gathered(slice(160 * block, 160 * (block + 1)), ROW - 1, ROW))
            .astype(BF16)
            .reshape(16, 5, 2, 128)
        )

    def post(to):
        pltpu.make_async_remote_copy(
            src_ref=sendbuf.at[to],
            dst_ref=recv.at[my_seq],
            send_sem=out_send,
            recv_sem=out_recv,
            device_id=(to, my_row),
            device_id_type=MESH,
        ).start()

    every_other(post)
    recv[my_seq] = sendbuf[my_seq]

    for t in range(3):
        pltpu.make_async_copy(taps.at[t], taps.at[t], tap_sem.at[t]).wait()
    arrived = recv.at[pl.ds(0, SEQ - 1)]
    pltpu.make_async_copy(arrived, arrived, out_recv).wait()
    left = iota((160, 128), 1) < 64
    for block in range(4):
        got = recv[16 * block : 16 * (block + 1)].reshape(160, 128).astype(F32)
        turned = pltpu.roll(got, 64, 1)
        parts = jnp.concatenate(
            [
                jnp.where(left, got, 0.0),
                jnp.where(left, turned, 0.0),
                jnp.where(left, 0.0, turned),
                jnp.where(left, 0.0, got),
            ],
            axis=0,
        ).astype(BF16)
        y[:, 16 * block : 16 * (block + 1), :] = (
            dot(mover[...], parts).astype(BF16).reshape(16, 16, 128)
        )

    rows = CAP * SEQ
    column = lax.rem(iota((rows, 128), 0), SEQ)
    lane = iota((rows, 128), 1)

    def rims(v):
        right = jnp.where(column == SEQ - 1, 0.0, pltpu.roll(v, rows - 1, 0))
        left = jnp.where(column == 0, 0.0, pltpu.roll(v, 1, 0))
        return jnp.where(lax.rem(lane, 64) < 32, right, left)

    wide = [y[CAP * t : CAP * (t + 1)].reshape(rows, 128).astype(F32) for t in range(4)]
    around = [rims(v) for v in wide]
    first_col = iota((SEQ, C), 0) == 0
    last_col = iota((SEQ, C), 0) == SEQ - 1
    xs = []
    for t in range(3):
        xs.append(
            jnp.concatenate(
                [wide[t], jnp.where(lane < 64, around[t], wide[t + 1]), around[t + 1]], axis=1
            ).astype(BF16)
        )

    def features(t):
        for p in range(2):
            cols = slice(2 * p * C, 2 * (p + 1) * C)
            feat[t, :, cols] = dot(xs[t], w1[:, cols])

    def activate(t):
        for k in range(CAP):
            live = 0.5 * mask[5 * k + t + 2 : 5 * k + t + 3, 0:1]
            here = slice(k * SEQ, (k + 1) * SEQ)
            for p in range(2):
                for r in range(2):
                    v = feat[t, here, (2 * p + r) * C : (2 * p + r + 1) * C] + bias1_row
                    factor = lax.rsqrt(jnp.mean(v * v, axis=1, keepdims=True) + EPSILON) * live
                    n = v * factor * gain_row
                    a = n + n * jnp.tanh(n)

                    def put(side, e, value):
                        lhs[
                            t,
                            side * rows + k * SEQ : side * rows + (k + 1) * SEQ,
                            (3 * p + e) * C : (3 * p + e + 1) * C,
                        ] = value.astype(BF16)

                    if r == 0:
                        put(0, 1, a)
                        put(1, 0, a)
                        put(1, 2, jnp.where(last_col, 0.0, pltpu.roll(a, SEQ - 1, 0)))
                    else:
                        put(0, 2, a)
                        put(1, 1, a)
                        put(0, 0, jnp.where(first_col, 0.0, pltpu.roll(a, 1, 0)))

    features(0)
    activate(0)
    for t in range(2):
        features(t + 1)
        product = dot(lhs[t], taps[t])
        if t == 0:
            acc[...] = product
        else:
            acc[...] += product
        activate(t + 1)

    both_bias = bias2[...].reshape(1, C) + bias1_row
    for n in range(3):
        products = [
            dot(lhs[2, r * rows : (r + 1) * rows, :], taps[2, :, 256 * n : 256 * (n + 1)])
            for r in range(2)
        ]
        for part in range(2):
            at = 2 * n + part
            i, at_c = at // 3, 128 * (at % 3)
            for k in range(CAP):
                live = mask[5 * k + 4 : 5 * k + 5, 0:1]
                for r in range(2):
                    here = slice(r * rows + k * SEQ, r * rows + (k + 1) * SEQ)
                    col = (2 * i + r) * C + at_c
                    mix[part, k, pl.ds(r, SEQ, stride=2), :] = (
                        products[r][k * SEQ : (k + 1) * SEQ, 128 * part : 128 * (part + 1)]
                        + acc[here, 128 * at : 128 * (at + 1)]
                        + feat[2, k * SEQ : (k + 1) * SEQ, col : col + 128]
                        + both_bias[:, at_c : at_c + 128]
                    ) * live
                out[k, i, :, at_c : at_c + 128] = mix[part, k].astype(BF16)

    for copy in share_copies + stat_copies + tok_copies:
        copy.wait_send()
    sent = sendbuf.at[pl.ds(0, SEQ - 1)]
    pltpu.make_async_copy(sent, sent, out_send).wait()


def shards(
    hidden,
    modulation,
    projection,
    projection_bias,
    input_kernel,
    input_bias,
    norm_gain,
    block_kernel,
    block_bias,
    frame_counts,
    decoder_plan,
):
    hbm = pl.BlockSpec(memory_space=pltpu.HBM)
    return pl.pallas_call(
        kernel,
        out_shape=jax.ShapeDtypeStruct((CAP, 2, 2 * SEQ, C), BF16),
        in_specs=[hbm] * 11,
        out_specs=pl.BlockSpec(memory_space=pltpu.VMEM),
        scratch_shapes=[
            pltpu.VMEM((FRAMES, DL), BF16),
            pltpu.VMEM((2, REQ, DL), F32),
            pltpu.VMEM((4 * Z, DL), BF16),
            pltpu.VMEM((1, 4 * Z), F32),
            pltpu.VMEM((1, REQ), jnp.int32),
            pltpu.VMEM((1, FRAMES), jnp.int32),
            pltpu.VMEM((27, Z, C), BF16),
            pltpu.VMEM((C,), F32),
            pltpu.VMEM((C,), F32),
            pltpu.VMEM((C,), F32),
            pltpu.VMEM((2 * ROW, QF), F32),
            pltpu.VMEM((ROW - 1, 2 * ROW, QF), F32),
            pltpu.VMEM((DL, 128), BF16),
            pltpu.VMEM((4 * REQ, DL), BF16),
            pltpu.VMEM((REQ, 128), F32),
            pltpu.VMEM((REQ, 128), BF16),
            pltpu.VMEM((ROW - 1, REQ, 128), BF16),
            pltpu.VMEM((ROW, QF // 2, 128), F32),
            pltpu.VMEM((ROW, QF // 2, 128), F32),
            pltpu.VMEM((ROW, QF // 2, 128), F32),
            pltpu.VMEM((ROW, QF // 2, 128), BF16),
            pltpu.VMEM((ROW - 1, ROW, QF // 2, 128), BF16),
            pltpu.VMEM((2 * FRAMES, 128), BF16),
            pltpu.VMEM((10 * SEQ, 2 * FRAMES), BF16),
            pltpu.VMEM((SEQ, 5, 2, 128), BF16),
            pltpu.VMEM((SEQ, 5, 2, 128), BF16),
            pltpu.VMEM((16, SEQ, 128), BF16),
            pltpu.VMEM((256, 640), BF16),
            pltpu.VMEM((24, 128), F32),
            pltpu.VMEM((3, 6 * C, 2 * C), BF16),
            pltpu.VMEM((24 * Z, 4 * C), BF16),
            pltpu.VMEM((3, 2 * CAP * SEQ, 6 * C), BF16),
            pltpu.VMEM((2 * CAP * SEQ, 2 * C), F32),
            pltpu.VMEM((3, CAP * SEQ, 4 * C), F32),
            pltpu.VMEM((2, CAP, 2 * SEQ, 128), F32),
            pltpu.SemaphoreType.DMA((10 + ROW,)),
            pltpu.SemaphoreType.DMA((ROW - 1,)),
            pltpu.SemaphoreType.DMA((ROW - 1,)),
            pltpu.SemaphoreType.DMA((ROW - 1,)),
            pltpu.SemaphoreType.DMA((ROW - 1,)),
            pltpu.SemaphoreType.DMA((ROW, ROW - 1)),
            pltpu.SemaphoreType.DMA((ROW, ROW - 1)),
            pltpu.SemaphoreType.DMA,
            pltpu.SemaphoreType.DMA,
            pltpu.SemaphoreType.DMA((3,)),
        ],
        compiler_params=pltpu.CompilerParams(
            collective_id=0, has_side_effects=True, vmem_limit_bytes=44 << 20
        ),
    )(*[pltpu.with_memory_space_constraint(x, pltpu.HBM) for x in (
        hidden.reshape(FRAMES, DL),
        modulation,
        projection.T,
        projection_bias.reshape(1, 4 * Z),
        input_kernel,
        input_bias,
        norm_gain,
        block_kernel,
        block_bias,
        frame_counts.reshape(1, REQ),
        decoder_plan.reshape(1, FRAMES),
    )])


def solution(mesh):
    placed = (
        P(None, "seq", "row"),
        P(None, None, "row"),
        P("row", None),
        P(),
        P(),
        P(),
        P(),
        P(),
        P(),
        P(),
        P(),
    )
    return jax.shard_map(
        shards,
        mesh=mesh,
        in_specs=placed,
        out_specs=P(("seq", "row"), None, None, None),
        check_vma=False,
    )
```
